256 devices in a mesh: tile: 128 (over z, x_lo, y, core), lev: 2 (over x_hi).
Axes of the slice: x: 4 (x_hi: 2, x_lo: 2; x = x_hi * 2 + x_lo), y: 4, z: 8, core: 2. Of those that a mesh axis runs over, the one named last changes fastest.
Arguments:
- tracers: float32 [2, 2048, 64, 384], P(None, 'tile', 'lev'), may hold values from -6 to 6
- zonal_courant: float32 [2048, 64, 384], P('tile', 'lev'), may hold values from -0.9 to 0.9
- merid_courant: float32 [2048, 64, 384], P('tile', 'lev'), may hold values from -0.9 to 0.9
- vertical_courant: float32 [2048, 64, 384], P('tile', 'lev'), may hold values from -0.9 to 0.9
- diffusivity: float32 [2048, 64, 384], P('tile', 'lev'), may hold values from 0.05 to 0.5
- turbulence: float32 [2048, 64, 384], P('tile', 'lev'), may hold values from 4 to 4000000
- sea_column: int32 [2048, 384], P('tile'), may hold values 0 or 1
- bottom_level: int32 [2048, 384], P('tile'), may hold values from 0 to 63
Outputs:
- updated: float32 [2, 2048, 64, 384], P(None, 'tile', 'lev')
The draws below stay inside these ranges and needn't reach their ends.
All inputs are finite; a program needn't handle non-finite values. No bound on the sum of `sea_column` on one device may be relied on, other than what follows from the above.
Results may differ from the reference program's by a relative error of at most 0.0003.
Values sent between devices are 32-bit elements; how exact they have to be, the bound alone decides.
No kernel may reach another device: no remote copies, remote signals or barrier semaphores. Data moves between devices by JAX's collectives and lax.ppermute only.
A program may use at most 64 MiB of HBM per device.

```python
import math
import jax
import jax.numpy as jnp
from jax import lax

NY = 384
NX = 2048
NZ = 64


def place_ends(entries, stream_key, least, top_value):
    index_at = [jax.random.randint(jax.random.fold_in(stream_key, axis), (), 0, length) for axis, length in enumerate(entries.shape)]
    widest = entries.shape.index(max(entries.shape))
    next_to = index_at[:widest] + [(index_at[widest] + 1) % entries.shape[widest]] + index_at[widest + 1:]
    return entries.at[tuple(index_at)].set(least).at[tuple(next_to)].set(top_value)


def shard_levels(rng, dims, cuts, low, high):
    loudness = 1.0
    for dim, parts in cuts:
        draws = jax.random.uniform(jax.random.fold_in(jax.random.fold_in(rng, 6), dim), (parts,), jnp.float32, low / len(cuts), high / len(cuts))
        loudness = loudness * jnp.repeat(jnp.exp(draws), dims[dim] // parts).reshape((-1,) + (1,) * (len(dims) - 1 - dim))
    return loudness


def gaussian(own_key, extent, scale, limit, cuts=(), kind=jnp.bfloat16):
    array = jax.random.normal(own_key, extent, jnp.float32) * scale
    if len(cuts) > 0:
        array = shard_levels(own_key, extent, cuts, -0.22, 0.18) * array
    return jnp.clip(array, min=-limit, max=limit).astype(kind)


def setup_inputs(seed: int = 0) -> dict:
    key_of = jax.random.split(jax.random.key(seed), 9)
    return {
        "tracers": gaussian(key_of[0], (2, NX, NZ, NY), 1.0, 6.0, ((1, 128), (2, 2)), jnp.float32),
        "zonal_courant": jnp.clip(jax.random.uniform(key_of[1], (NX, NZ, NY), jnp.float32, -0.9, 0.9) * shard_levels(key_of[1], (NX, NZ, NY), ((0, 128), (1, 2)), -0.4, 0.0), -0.9, 0.9),
        "merid_courant": jnp.clip(jax.random.uniform(key_of[2], (NX, NZ, NY), jnp.float32, -0.9, 0.9) * shard_levels(key_of[2], (NX, NZ, NY), ((0, 128), (1, 2)), -0.4, 0.0), -0.9, 0.9),
        "vertical_courant": jnp.clip(jax.random.uniform(key_of[3], (NX, NZ, NY), jnp.float32, -0.9, 0.9) * shard_levels(key_of[3], (NX, NZ, NY), ((0, 128), (1, 2)), -0.4, 0.0), -0.9, 0.9),
        "diffusivity": jnp.clip(jnp.exp(math.log(0.5) - 2.3025851 * jax.random.uniform(key_of[4], (NX, NZ, NY), jnp.float32) ** shard_levels(key_of[4], (NX, NZ, NY), ((0, 128), (1, 2)), -0.2, 0.2)), 0.05, 0.5),
        "turbulence": jnp.clip(jnp.exp(math.log(4000000) - 13.815511 * jax.random.uniform(key_of[5], (NX, NZ, NY), jnp.float32) ** shard_levels(key_of[5], (NX, NZ, NY), ((0, 128), (1, 2)), -0.2, 0.2)), 4.0, 4000000),
        "sea_column": place_ends((jax.random.randint(key_of[6], (NX, NY), 0, 5) < 4).astype(jnp.int32), jax.random.fold_in(key_of[6], 1), 0, 1),
        "bottom_level": place_ends(jax.random.randint(key_of[7], (NX, NY), 0, NZ), jax.random.fold_in(key_of[7], 1), 0, NZ - 1).astype(jnp.int32),
    }


thermal_coef = 0.2
haline_coef = 0.8
taper_eps = 0.05

def shift_north(values):
    return jnp.concatenate([values[..., 1:], jnp.zeros_like(values[..., :1])], axis=-1)

def shift_south(values):
    return jnp.concatenate([jnp.zeros_like(values[..., :1]), values[..., :-1]], axis=-1)

def superbee(upwind, local_grad):
    larger = jnp.maximum(jnp.minimum(2.0 * jnp.abs(upwind), jnp.abs(local_grad)), jnp.minimum(jnp.abs(upwind), 2.0 * jnp.abs(local_grad)))
    return jnp.where(upwind * local_grad > 0.0, jnp.where(local_grad > 0.0, larger, -larger), 0.0)

def face_flux(courant, behind, in_front, grad_here, grad_back, grad_front):
    upwind = jnp.where(courant > 0.0, grad_back, grad_front)
    limited = superbee(upwind, grad_here)
    abs_speed = jnp.abs(courant)
    return courant * 0.5 * (behind + in_front) - 0.5 * abs_speed * (grad_here - (1.0 - abs_speed) * limited)

def isoneutral(grad_side, grad_vert, face_coeff):
    dens_side = haline_coef * grad_side[1] - thermal_coef * grad_side[0]
    dens_vert = haline_coef * grad_vert[1] - thermal_coef * grad_vert[0]
    slope_ratio = dens_side * dens_vert / (dens_vert * dens_vert + taper_eps)
    return face_coeff * (grad_side - slope_ratio * grad_vert)

def provisional(padded, cell_mask, east_courant, east_coeff, north_courant, coeff_own, down_courant):
    span_x = padded.shape[1] - 4
    span_z = padded.shape[2] - 4
    vert_mask = cell_mask[:, 1:] * cell_mask[:, :-1]
    vert_grad = vert_mask * (padded[:, :, 1:] - padded[:, :, :-1])
    centred = 0.5 * (vert_grad[:, :, 2:span_z + 2] + vert_grad[:, :, 1:span_z + 1])
    level_rows = padded[:, :, 2:span_z + 2]
    level_mask_rows = cell_mask[:, 2:span_z + 2]
    zonal_mask = level_mask_rows[1:] * level_mask_rows[:-1]
    zonal_grad = zonal_mask * (level_rows[:, 1:] - level_rows[:, :-1])
    face_mask = zonal_mask[1:span_x + 2]
    grad_here = zonal_grad[:, 1:span_x + 2]
    zonal_adv = face_flux(east_courant * face_mask, level_rows[:, 1:span_x + 2], level_rows[:, 2:span_x + 3], grad_here, zonal_grad[:, 0:span_x + 1], zonal_grad[:, 2:span_x + 3])
    zonal_vert = 0.5 * (centred[:, 1:span_x + 2] + centred[:, 2:span_x + 3])
    zonal_net = isoneutral(grad_here, zonal_vert, east_coeff * face_mask) - zonal_adv
    tendency = zonal_net[:, 1:] - zonal_net[:, :-1]
    own_rows = level_rows[:, 2:span_x + 2]
    own_mask = level_mask_rows[2:span_x + 2]
    merid_mask = own_mask * shift_north(own_mask)
    merid_grad = merid_mask * (shift_north(own_rows) - own_rows)
    merid_adv = face_flux(shift_north(north_courant) * merid_mask, own_rows, shift_north(own_rows), merid_grad, shift_south(merid_grad), shift_north(merid_grad))
    own_vert = centred[:, 2:span_x + 2]
    merid_vert = 0.5 * (own_vert + shift_north(own_vert))
    merid_net = isoneutral(merid_grad, merid_vert, shift_north(coeff_own) * merid_mask) - merid_adv
    tendency = tendency + merid_net - shift_south(merid_net)
    column_rows = padded[:, 2:span_x + 2]
    column_grad = vert_grad[:, 2:span_x + 2]
    column_mask = vert_mask[2:span_x + 2]
    vert_adv = face_flux(down_courant[:, 2:span_z + 3] * column_mask[:, 1:span_z + 2], column_rows[:, :, 1:span_z + 2], column_rows[:, :, 2:span_z + 3], column_grad[:, :, 1:span_z + 2], column_grad[:, :, 0:span_z + 1], column_grad[:, :, 2:span_z + 3])
    tendency = tendency - (vert_adv[:, :, 1:] - vert_adv[:, :, :-1])
    return own_rows + tendency

def level_mask(depth_rows, first_level, level_total):
    levels = (first_level + jnp.arange(level_total, dtype=jnp.int32)).astype(jnp.float32)
    inside = (levels[None, :, None] >= 0.0) & (levels[None, :, None] < depth_rows[:, None, :])
    return inside.astype(jnp.float32)

def thomas(lower_band, diagonal, upper_band, right_side):
    low_rows = jnp.moveaxis(lower_band, 1, 0)
    diag_rows = jnp.moveaxis(diagonal, 1, 0)
    up_rows = jnp.moveaxis(upper_band, 1, 0)
    rhs_rows = jnp.moveaxis(right_side, 2, 0)

    def forward(carried, pieces):
        ratio_prev, value_prev = carried
        low_row, diag_row, up_row, rhs_row = pieces
        pivot_row = diag_row - low_row * ratio_prev
        ratio_new = up_row / pivot_row
        value_new = (rhs_row - low_row * value_prev) / pivot_row
        return ((ratio_new, value_new), (ratio_new, value_new))
    initial = (jnp.zeros_like(diag_rows[0]), jnp.zeros_like(rhs_rows[0]))
    final_state, (ratios, values) = lax.scan(forward, initial, (low_rows, diag_rows, up_rows, rhs_rows))

    def backward(later_row, pieces):
        ratio_row, value_row = pieces
        result = value_row - ratio_row * later_row
        return (result, result)
    final_back, solved = lax.scan(backward, jnp.zeros_like(rhs_rows[0]), (ratios, values), reverse=True)
    return jnp.moveaxis(solved, 0, 2)

def reference(tracers, zonal_courant, merid_courant, vertical_courant, diffusivity, turbulence, sea_column, bottom_level):
    depth_rows = (sea_column * (bottom_level + 1)).astype(jnp.float32)
    wrapped = jnp.concatenate([tracers[:, -2:], tracers, tracers[:, :2]], axis=1)
    padded = jnp.pad(wrapped, ((0, 0), (0, 0), (2, 2), (0, 0)))
    depth_wrapped = jnp.concatenate([depth_rows[-2:], depth_rows, depth_rows[:2]], axis=0)
    cell_mask = level_mask(depth_wrapped, -2, NZ + 4)
    east_courant = jnp.concatenate([zonal_courant, zonal_courant[:1]], axis=0)
    east_coeff = jnp.concatenate([diffusivity, diffusivity[:1]], axis=0)
    down_courant = jnp.pad(vertical_courant, ((0, 0), (2, 2), (0, 0)))
    stepped = provisional(padded, cell_mask, east_courant, east_coeff, merid_courant, diffusivity, down_courant)
    own_mask = cell_mask[2:-2]
    face_rate = own_mask[:, 2:-2] * own_mask[:, 3:-1] * jnp.sqrt(turbulence)
    rate_above = jnp.concatenate([jnp.zeros_like(face_rate[:, :1]), face_rate[:, :-1]], axis=1)
    return thomas(-rate_above, 1.0 + rate_above + face_rate, -face_rate, stepped)
```

```python
import jax
import jax.numpy as jnp
from jax import lax
from jax.experimental import pallas as pl
from jax.experimental.pallas import tpu as pltpu
from jax.sharding import PartitionSpec as P

thermal_coef = 0.2
haline_coef = 0.8
taper_eps = 0.05

X = 16
K = 32
Y = 384
LANES = 3
FAR = 1 << 20
F32 = jnp.float32


def any_spec():
    return pl.BlockSpec(memory_space=pl.ANY)


def vmem_spec():
    return pl.BlockSpec(memory_space=pltpu.VMEM)


def run_copies(copies):
    for copy in copies:
        copy.start()
    for copy in copies:
        copy.wait()


def face_flux(courant, behind, in_front, grad, back, front):
    half = 0.5 * courant
    speed = jnp.abs(courant)
    half_speed = jnp.abs(half)
    weight = half_speed * (1.0 - speed)
    forward = courant > 0.0
    fluxes = []
    for t in range(2):
        upwind = jnp.where(forward, back[t], front[t])
        rising = grad[t] > 0.0
        size = jnp.abs(grad[t])
        along = jnp.where(rising, upwind, -upwind)
        limited = jnp.maximum(
            jnp.minimum(2.0 * jnp.minimum(size, along), jnp.maximum(size, along)), 0.0
        )
        limited = jnp.where(rising, limited, -limited)
        fluxes.append(half * (behind[t] + in_front[t]) - half_speed * grad[t] + weight * limited)
    return fluxes


def isoneutral(grad, vert, coeff):
    dens_side = haline_coef * grad[1] - thermal_coef * grad[0]
    dens_vert = haline_coef * vert[1] - thermal_coef * vert[0]
    slope = dens_side * dens_vert / (dens_vert * dens_vert + taper_eps)
    return [coeff * (grad[t] - slope * vert[t]) for t in range(2)]


def lane_roll(values, shift):
    return pltpu.roll(values, shift % Y, 1)


def row_roll(values, shift):
    return pltpu.roll(values, shift % values.shape[0], 0)


def south_depth(depth):
    lane = lax.broadcasted_iota(jnp.int32, depth.shape, 1)
    return jnp.where(lane == 0, 0, jnp.minimum(depth, lane_roll(depth, 1)))


def west_depth(depth):
    return jnp.minimum(depth, row_roll(depth, 1))


def pack_kernel(
    tracers, zonal, vertical, diffusivity, turbulence, sea, bottom,
    east_msg, west_msg, level_msg, east_corner, west_corner, depth_rows, sems
):
    slab = lax.axis_index("lev")
    edge = (K - 1) * (1 - slab)
    first = (K - 2) * (1 - slab)
    copies = []

    def add(src, dst):
        copies.append(pltpu.make_async_copy(src, dst, sems.at[len(copies)]))
        copies[-1].start()

    for t in range(2):
        for i in range(2):
            rows = pl.ds((2 * t + i) * K, K)
            add(tracers.at[t, X - 2 + i], east_msg.at[rows])
            add(tracers.at[t, i], west_msg.at[rows])
            add(tracers.at[t, :, first + i, :], level_msg.at[2 * t + i])
        add(tracers.at[t, X - 1, edge, :], east_corner.at[t])
        add(tracers.at[t, 0, edge, :], west_corner.at[t])
    add(zonal.at[0], west_msg.at[pl.ds(4 * K, K)])
    add(diffusivity.at[0], west_msg.at[pl.ds(5 * K, K)])
    fifth = len(copies)
    upper = pltpu.make_async_copy(turbulence.at[:, K - 1, :], level_msg.at[4], sems.at[fifth])
    lower = pltpu.make_async_copy(vertical.at[:, 0, :], level_msg.at[4], sems.at[fifth])

    @pl.when(slab == 0)
    def _():
        upper.start()

    @pl.when(slab == 1)
    def _():
        lower.start()

    depth_rows[...] = (sea[...] * (bottom[...] + 1)).astype(F32)
    last = [
        pltpu.make_async_copy(depth_rows.at[pl.ds(8, 8)], east_msg.at[pl.ds(4 * K, 8)], sems.at[fifth + 1]),
        pltpu.make_async_copy(depth_rows.at[pl.ds(0, 8)], west_msg.at[pl.ds(6 * K, 8)], sems.at[fifth + 2]),
    ]
    for copy in last:
        copy.start()
    upper.wait()
    for copy in copies + last:
        copy.wait()


def interior_kernel(
    tracers, zonal, merid, vertical, diffusivity, turbulence, sea, bottom,
    p_out, inverse_out, carry_out, ratio_out, tail_out,
    q, zc, mc, vc, df, tb, below_flux, rate, sems
):
    slab = lax.axis_index("lev")
    edge = (K - 1) * (1 - slab)
    base = K * slab

    def copies(k):
        pairs = [
            (tracers.at[0, :, k, :], q.at[0, k]),
            (tracers.at[1, :, k, :], q.at[1, k]),
            (zonal.at[:, k, :], zc.at[k]),
            (merid.at[:, k, :], mc.at[k]),
            (vertical.at[:, k, :], vc.at[k]),
            (diffusivity.at[:, k, :], df.at[k]),
            (turbulence.at[:, k, :], tb.at[k]),
        ]
        return [pltpu.make_async_copy(a, b, sems.at[i, k]) for i, (a, b) in enumerate(pairs)]

    @pl.loop(0, K)
    def _(k):
        for copy in copies(k):
            copy.start()

    depth = sea[...] * (bottom[...] + 1)
    depth_west = west_depth(depth)
    row = lax.broadcasted_iota(jnp.int32, (X, Y), 0)
    depth_west_inner = jnp.where((row >= 2) & (row <= X - 2), depth_west, 0)
    depth_south = south_depth(depth)
    below_flux[...] = jnp.zeros_like(below_flux)
    rate[0] = jnp.zeros((X, Y), F32)

    for k in range(2):
        for copy in copies(k):
            copy.wait()

    @pl.loop(0, K)
    def _(k):
        ahead = jnp.minimum(k + 2, K - 1)

        @pl.when(k + 2 < K)
        def _():
            for copy in copies(ahead):
                copy.wait()

        level = base + k
        up = jnp.maximum(k - 1, 0)
        down = jnp.minimum(k + 1, K - 1)
        here = [q[t, k] for t in range(2)]
        next_row = [q[t, down] for t in range(2)]
        open_up = jnp.where(k > 0, level, FAR) < depth
        open_down = jnp.where(k < K - 1, level + 1, FAR) < depth
        open_far = jnp.where(k < K - 2, level + 2, FAR) < depth
        grad_up = [jnp.where(open_up, here[t] - q[t, up], 0.0) for t in range(2)]
        grad_down = [jnp.where(open_down, next_row[t] - here[t], 0.0) for t in range(2)]
        grad_far = [jnp.where(open_far, q[t, ahead] - next_row[t], 0.0) for t in range(2)]
        centred = [0.5 * (grad_up[t] + grad_down[t]) for t in range(2)]
        known = jnp.where(slab == 0, k < K - 2, k > 0)
        open_flux = jnp.where(known, level + 1, FAR) < depth
        down_courant = jnp.where(open_flux, vc[down], 0.0)
        vert = face_flux(down_courant, here, next_row, grad_down, grad_up, grad_far)
        total = []
        for t in range(2):
            total.append(here[t] + below_flux[t] - vert[t])
            below_flux[t] = vert[t]
        rate[k + 1] = jnp.where(level + 1 < depth, jnp.sqrt(tb[k]), 0.0)
        iso_level = jnp.where(k == edge, FAR, level)
        spread = df[k]

        open_west = level < depth_west
        behind = [row_roll(here[t], 1) for t in range(2)]
        grad = [jnp.where(open_west, here[t] - behind[t], 0.0) for t in range(2)]
        flux = face_flux(
            jnp.where(level < depth_west_inner, zc[k], 0.0),
            behind,
            here,
            grad,
            [row_roll(grad[t], 1) for t in range(2)],
            [row_roll(grad[t], -1) for t in range(2)],
        )
        iso = isoneutral(
            grad,
            [0.5 * (centred[t] + row_roll(centred[t], 1)) for t in range(2)],
            jnp.where(iso_level < depth_west_inner, spread, 0.0),
        )
        for t in range(2):
            net = iso[t] - flux[t]
            total[t] = total[t] + (row_roll(net, -1) - net)

        open_south = level < depth_south
        behind = [lane_roll(here[t], 1) for t in range(2)]
        grad = [jnp.where(open_south, here[t] - behind[t], 0.0) for t in range(2)]
        flux = face_flux(
            jnp.where(open_south, mc[k], 0.0),
            behind,
            here,
            grad,
            [lane_roll(grad[t], 1) for t in range(2)],
            [lane_roll(grad[t], -1) for t in range(2)],
        )
        iso = isoneutral(
            grad,
            [0.5 * (centred[t] + lane_roll(centred[t], 1)) for t in range(2)],
            jnp.where(iso_level < depth_south, spread, 0.0),
        )
        for t in range(2):
            net = iso[t] - flux[t]
            total[t] = total[t] + (lane_roll(net, -1) - net)
            for lane in range(LANES):
                p_out[t, lane, pl.ds(k * X, X), :] = total[t][:, lane * 128 : lane * 128 + 128]

    def eliminate(j, tail):
        prev_face = jnp.where(slab == 0, j, K - j)
        next_face = jnp.where(slab == 0, j + 1, K - 1 - j)
        k = jnp.where(slab == 0, j, K - 1 - j)
        prev_rate = rate[prev_face]
        next_rate = rate[next_face]
        rest = 1.0 + prev_rate * tail
        inverse = 1.0 / (rest + next_rate)
        inverse_out[k] = inverse
        carry_out[k] = prev_rate * inverse
        ratio_out[k] = next_rate * inverse
        return rest * inverse

    tail_out[0] = lax.fori_loop(0, K - 1, eliminate, jnp.zeros((X, Y), F32))
    tail_out[1] = rate[jnp.where(slab == 0, K - 1, 1)]


def edge_kernel(
    east_msg, west_msg, level_msg, east_corner, west_corner,
    tracers, zonal, vertical, diffusivity, turbulence, sea, bottom,
    p_in, inverse, carry, tail,
    v_out, meet_out,
    p, cols, zcols, dcols, rows, vrows, drow, trow, sems
):
    slab = lax.axis_index("lev")
    edge = (K - 1) * (1 - slab)
    inner = 30 - 29 * slab
    first = (K - 3) * (1 - slab)
    base = K * slab
    copies = []

    def add(src, dst):
        copies.append(pltpu.make_async_copy(src, dst, sems.at[len(copies)]))

    own = (0, 1, 2, X - 3, X - 2, X - 1)
    for t in range(2):
        for i, x in enumerate(own):
            add(tracers.at[t, x], cols.at[t, i])
        for i in range(3):
            add(tracers.at[t, :, first + i, :], rows.at[t, 2 * slab + i])
    for i, x in enumerate((0, 1, X - 1)):
        add(zonal.at[x], zcols.at[i])
        add(diffusivity.at[x], dcols.at[i])
    add(vertical.at[:, edge, :], vrows.at[0])
    add(vertical.at[:, 1, :], vrows.at[1])
    add(diffusivity.at[:, edge, :], drow)
    add(turbulence.at[:, K - 1, :], trow)
    add(p_in, p)
    run_copies(copies)
    for t in range(2):
        for i in range(2):
            rows[t, 3 * (1 - slab) + i] = level_msg[2 * t + i]

    depth = sea[...] * (bottom[...] + 1)

    level = base + lax.broadcasted_iota(jnp.int32, (K, Y), 0)
    local_row = lax.broadcasted_iota(jnp.int32, (K, Y), 0)

    def zonal_edge(q, depths, halo, courants, spreads):
        centred = []
        for i in range(3):
            column_depth = depths[i + 1]
            pair = []
            for t in range(2):
                mine = q[t][i + 1]
                outer = halo[t][i]
                below = jnp.where(local_row == K - 1, outer, row_roll(mine, -1))
                down = jnp.where(level + 1 < column_depth, below - mine, 0.0)
                top = jnp.where(
                    (slab == 1) & (level < column_depth), mine - outer, 0.0
                )
                up = jnp.where(local_row == 0, top, row_roll(down, 1))
                pair.append(0.5 * (up + down))
            centred.append(pair)
        opened = [level < jnp.minimum(depths[i], depths[i + 1]) for i in range(4)]
        grads = [
            [jnp.where(opened[i], q[t][i + 1] - q[t][i], 0.0) for t in range(2)] for i in range(4)
        ]
        nets = []
        for f in range(2):
            flux = face_flux(
                jnp.where(opened[f + 1], courants[f], 0.0),
                [q[t][f + 1] for t in range(2)],
                [q[t][f + 2] for t in range(2)],
                grads[f + 1],
                grads[f],
                grads[f + 2],
            )
            iso = isoneutral(
                grads[f + 1],
                [0.5 * (centred[f][t] + centred[f + 1][t]) for t in range(2)],
                jnp.where(opened[f + 1], spreads[f], 0.0),
            )
            nets.append([iso[t] - flux[t] for t in range(2)])
        return nets

    def add_column(t, x, values):
        for lane in range(LANES):
            where = (t, lane, pl.ds(x, K, stride=X), slice(None))
            p[where] = p[where] + values[:, lane * 128 : lane * 128 + 128]

    def depth_row(x):
        return depth[x : x + 1]

    def near(t, x):
        return level_msg[2 * t + slab, x : x + 1, :]

    west_depths = east_msg[4 * K : 4 * K + 8, :].astype(jnp.int32)
    nets = zonal_edge(
        [
            [east_msg[(2 * t + i) * K : (2 * t + i + 1) * K, :] for i in range(2)]
            + [cols[t, i] for i in range(3)]
            for t in range(2)
        ],
        [west_depths[6:7], west_depths[7:8], depth_row(0), depth_row(1), depth_row(2)],
        [[east_corner[t : t + 1, :], near(t, 0), near(t, 1)] for t in range(2)],
        [zcols[0], zcols[1]],
        [dcols[0], dcols[1]],
    )
    for t in range(2):
        add_column(t, 0, nets[1][t] - nets[0][t])
        add_column(t, 1, -nets[1][t])
    east_depths = west_msg[6 * K : 6 * K + 8, :].astype(jnp.int32)
    nets = zonal_edge(
        [
            [cols[t, 3 + i] for i in range(3)]
            + [west_msg[(2 * t + i) * K : (2 * t + i + 1) * K, :] for i in range(2)]
            for t in range(2)
        ],
        [depth_row(X - 3), depth_row(X - 2), depth_row(X - 1), east_depths[0:1], east_depths[1:2]],
        [[near(t, X - 2), near(t, X - 1), west_corner[t : t + 1, :]] for t in range(2)],
        [zcols[2], west_msg[4 * K : 5 * K, :]],
        [dcols[2], west_msg[5 * K : 6 * K, :]],
    )
    for t in range(2):
        add_column(t, X - 2, nets[0][t])
        add_column(t, X - 1, nets[1][t] - nets[0][t])

    start = K - 3 + slab
    q = [[rows[t, i] for i in range(5)] for t in range(2)]
    grads = [
        [jnp.where(start + i + 1 < depth, q[t][i + 1] - q[t][i], 0.0) for t in range(2)]
        for i in range(4)
    ]
    other = level_msg[4]
    courant_low = jnp.where(slab == 0, other, vrows[1])
    above = face_flux(
        jnp.where(start + 2 < depth, vrows[0], 0.0),
        [q[t][1] for t in range(2)], [q[t][2] for t in range(2)], grads[1], grads[0], grads[2],
    )
    under = face_flux(
        jnp.where(start + 3 < depth, courant_low, 0.0),
        [q[t][2] for t in range(2)], [q[t][3] for t in range(2)], grads[2], grads[1], grads[3],
    )
    centred = [0.5 * (grads[1][t] + grads[2][t]) for t in range(2)]
    here = [q[t][2] for t in range(2)]
    mid = start + 2
    depth_west = west_depth(depth)
    row = lax.broadcasted_iota(jnp.int32, (X, Y), 0)
    depth_west_inner = jnp.where((row >= 2) & (row <= X - 2), depth_west, 0)
    depth_south = south_depth(depth)
    spread = drow[...]
    grad = [jnp.where(mid < depth_west, here[t] - row_roll(here[t], 1), 0.0) for t in range(2)]
    zonal_iso = isoneutral(
        grad,
        [0.5 * (centred[t] + row_roll(centred[t], 1)) for t in range(2)],
        jnp.where(mid < depth_west_inner, spread, 0.0),
    )
    grad = [jnp.where(mid < depth_south, here[t] - lane_roll(here[t], 1), 0.0) for t in range(2)]
    merid_iso = isoneutral(
        grad,
        [0.5 * (centred[t] + lane_roll(centred[t], 1)) for t in range(2)],
        jnp.where(mid < depth_south, spread, 0.0),
    )

    def add_level(t, k, values):
        for lane in range(LANES):
            where = (t, lane, pl.ds(pl.multiple_of(k * X, X), X), slice(None))
            p[where] = p[where] + values[:, lane * 128 : lane * 128 + 128]

    for t in range(2):
        change = row_roll(zonal_iso[t], -1) - zonal_iso[t]
        change = change + (lane_roll(merid_iso[t], -1) - merid_iso[t])
        add_level(t, edge, change - (under[t] - above[t]))
        add_level(t, inner, jnp.where(slab == 0, -above[t], under[t]))

    def provisional(t, k):
        rows_at = pl.ds(pl.multiple_of(k * X, X), X)
        return jnp.concatenate([p[t, lane, rows_at, :] for lane in range(LANES)], axis=1)

    def forward(j, values):
        k = jnp.where(slab == 0, j, K - 1 - j)
        inv = inverse[k]
        car = carry[k]
        new = tuple(provisional(t, k) * inv + car * values[t] for t in range(2))
        for t in range(2):
            v_out[t, k] = new[t]
        return new

    zero = jnp.zeros((X, Y), F32)
    values = lax.fori_loop(0, K - 1, forward, (zero, zero))
    meet_rate = jnp.where(K < depth, jnp.sqrt(jnp.where(slab == 0, trow[...], other)), 0.0)
    prev_rate = tail[1]
    rest = 1.0 + prev_rate * tail[0]
    inv = 1.0 / (rest + meet_rate)
    for t in range(2):
        meet_out[t] = (provisional(t, edge) + prev_rate * values[t]) * inv
    meet_out[2] = rest * inv


def finish_kernel(v, ratio, mine, theirs, out, u, sems):
    slab = lax.axis_index("lev")
    own_tail = mine[2]
    scale = 1.0 / (own_tail + (1.0 - own_tail) * theirs[2])
    last = tuple((mine[t] + (1.0 - own_tail) * theirs[t]) * scale for t in range(2))
    edge = (K - 1) * (1 - slab)

    def copies(k):
        return [pltpu.make_async_copy(u.at[t, k], out.at[t, :, k, :], sems.at[t, k]) for t in range(2)]

    for t in range(2):
        u[t, edge] = last[t]
    for copy in copies(edge):
        copy.start()

    def backward(i, values):
        j = K - 2 - i
        k = jnp.where(slab == 0, j, K - 1 - j)
        rat = ratio[k]
        new = tuple(v[t, k] + rat * values[t] for t in range(2))
        for t in range(2):
            u[t, k] = new[t]
        for copy in copies(k):
            copy.start()
        return new

    lax.fori_loop(0, K - 1, backward, last)

    @pl.loop(0, K)
    def _(k):
        for copy in copies(k):
            copy.wait()


def shape(*dims):
    return jax.ShapeDtypeStruct(dims, F32)


def params():
    return pltpu.CompilerParams(vmem_limit_bytes=40 * 1024 * 1024)


def local(
    tracers, zonal, merid, vertical, diffusivity, turbulence, sea, bottom
):
    count = lax.axis_size("tile")
    east_msg, west_msg, level_msg, east_corner, west_corner = pl.pallas_call(
        pack_kernel,
        name="pack",
        in_specs=[any_spec()] * 5 + [vmem_spec()] * 2,
        out_specs=[any_spec()] * 5,
        out_shape=[
            shape(4 * K + 8, Y), shape(6 * K + 8, Y), shape(5, X, Y), shape(2, Y), shape(2, Y)
        ],
        scratch_shapes=[pltpu.VMEM((X, Y), F32), pltpu.SemaphoreType.DMA((24,))],
        compiler_params=params(),
    )(tracers, zonal, vertical, diffusivity, turbulence, sea, bottom)

    eastward = [(i, (i + 1) % count) for i in range(count)]
    east_cross = []
    west_cross = []
    for source, target in eastward:
        for slab in range(2):
            east_cross.append((2 * source + slab, 2 * target + 1 - slab))
            west_cross.append((2 * target + slab, 2 * source + 1 - slab))
    east_in = lax.ppermute(east_msg, "tile", eastward)
    west_in = lax.ppermute(west_msg, "tile", [(b, a) for a, b in eastward])
    level_in = lax.ppermute(level_msg, "lev", [(0, 1), (1, 0)])
    east_corner_in = lax.ppermute(east_corner, ("tile", "lev"), east_cross)
    west_corner_in = lax.ppermute(west_corner, ("tile", "lev"), west_cross)

    p, inverse, carry, ratio, tail = pl.pallas_call(
        interior_kernel,
        name="interior",
        in_specs=[any_spec()] * 6 + [vmem_spec()] * 2,
        out_specs=[vmem_spec()] * 5,
        out_shape=[
            shape(2, LANES, K * X, 128), shape(K, X, Y), shape(K, X, Y), shape(K, X, Y), shape(2, X, Y)
        ],
        scratch_shapes=[
            pltpu.VMEM((2, K, X, Y), F32),
            pltpu.VMEM((K, X, Y), F32),
            pltpu.VMEM((K, X, Y), F32),
            pltpu.VMEM((K, X, Y), F32),
            pltpu.VMEM((K, X, Y), F32),
            pltpu.VMEM((K, X, Y), F32),
            pltpu.VMEM((2, X, Y), F32),
            pltpu.VMEM((K + 1, X, Y), F32),
            pltpu.SemaphoreType.DMA((7, K)),
        ],
        compiler_params=params(),
        cost_estimate=pl.CostEstimate(flops=50_000_000, bytes_accessed=40_000_000, transcendentals=0),
    )(tracers, zonal, merid, vertical, diffusivity, turbulence, sea, bottom)

    v, meet = pl.pallas_call(
        edge_kernel,
        name="edges",
        in_specs=[vmem_spec()] * 5 + [any_spec()] * 5 + [vmem_spec()] * 2 + [any_spec()] + [vmem_spec()] * 3,
        out_specs=[vmem_spec()] * 2,
        out_shape=[shape(2, K, X, Y), shape(3, X, Y)],
        scratch_shapes=[
            pltpu.VMEM((2, LANES, K * X, 128), F32),
            pltpu.VMEM((2, 6, K, Y), F32),
            pltpu.VMEM((3, K, Y), F32),
            pltpu.VMEM((3, K, Y), F32),
            pltpu.VMEM((2, 5, X, Y), F32),
            pltpu.VMEM((2, X, Y), F32),
            pltpu.VMEM((X, Y), F32),
            pltpu.VMEM((X, Y), F32),
            pltpu.SemaphoreType.DMA((40,)),
        ],
        compiler_params=params(),
    )(
        east_in, west_in, level_in, east_corner_in, west_corner_in,
        tracers, zonal, vertical, diffusivity, turbulence, sea, bottom,
        p, inverse, carry, tail,
    )

    meet_in = lax.ppermute(meet, "lev", [(0, 1), (1, 0)])
    return pl.pallas_call(
        finish_kernel,
        name="finish",
        in_specs=[vmem_spec()] * 4,
        out_specs=any_spec(),
        out_shape=shape(2, X, K, Y),
        scratch_shapes=[pltpu.VMEM((2, K, X, Y), F32), pltpu.SemaphoreType.DMA((2, K))],
        compiler_params=params(),
    )(v, ratio, meet, meet_in)


def solution(mesh):
    return jax.shard_map(
        local,
        mesh=mesh,
        in_specs=(
            P(None, "tile", "lev", None),
            P("tile", "lev", None),
            P("tile", "lev", None),
            P("tile", "lev", None),
            P("tile", "lev", None),
            P("tile", "lev", None),
            P("tile", None),
            P("tile", None),
        ),
        out_specs=P(None, "tile", "lev", None),
        check_vma=False,
    )
```

```python
import jax
import jax.numpy as jnp
from jax import lax
from jax.experimental import pallas as pl
from jax.experimental.pallas import tpu as pltpu
from jax.sharding import PartitionSpec as P

thermal_coef = 0.2
haline_coef = 0.8
taper_eps = 0.05

X = 16
K = 32
Y = 384
LANES = 3
UNROLL = 2
AHEAD = 8
FAR = 1 << 20
F32 = jnp.float32


def any_spec():
    return pl.BlockSpec(memory_space=pl.ANY)


def vmem_spec():
    return pl.BlockSpec(memory_space=pltpu.VMEM)


def face_flux(courant, behind, grad, back, front):
    half = 0.5 * courant
    half_speed = jnp.abs(half)
    weight = half_speed - 2.0 * half_speed * half_speed
    lag = half - half_speed
    forward = courant > 0.0
    fluxes = []
    for t in range(2):
        upwind = jnp.where(forward, back[t], front[t])
        low = jnp.minimum(grad[t], 0.0)
        high = jnp.maximum(grad[t], 0.0)
        double = jnp.minimum(jnp.maximum(upwind + upwind, low), high)
        excess = jnp.minimum(jnp.maximum(upwind - grad[t], low), high)
        fluxes.append(courant * behind[t] + lag * grad[t] + weight * (double + excess))
    return fluxes


def reciprocal(values):
    guess = pl.reciprocal(values, approx=True)
    return guess * (2.0 - values * guess)


def isoneutral(grad, vert, coeff):
    ratio = haline_coef / thermal_coef
    dens_side = ratio * grad[1] - grad[0]
    dens_vert = ratio * vert[1] - vert[0]
    floor = 16.0 * taper_eps / (thermal_coef * thermal_coef)
    slope = dens_side * dens_vert * reciprocal(dens_vert * dens_vert + floor)
    return [coeff * (grad[t] - slope * vert[t]) for t in range(2)]


def lane_roll(values, shift):
    return pltpu.roll(values, shift % Y, 1)


def row_roll(values, shift):
    return pltpu.roll(values, shift % values.shape[0], 0)


def south_depth(depth):
    lane = lax.broadcasted_iota(jnp.int32, depth.shape, 1)
    return jnp.where(lane == 0, 0, jnp.minimum(depth, lane_roll(depth, 1)))


def west_depth(depth):
    return jnp.minimum(depth, row_roll(depth, 1))


def pack_kernel(
    tracers, zonal, vertical, diffusivity, turbulence, sea, bottom,
    east_msg, west_msg, level_msg, depth_rows, sems
):
    slab = lax.axis_index("lev")
    first = (K - 2) * (1 - slab)
    copies = []

    def add(src, dst):
        copies.append(pltpu.make_async_copy(src, dst, sems.at[len(copies)]))
        copies[-1].start()

    for t in range(2):
        for i in range(2):
            rows = pl.ds((2 * t + i) * K, K)
            add(tracers.at[t, X - 2 + i], east_msg.at[rows])
            add(tracers.at[t, i], west_msg.at[rows])
            add(tracers.at[t, :, first + i, :], level_msg.at[2 * t + i])
    add(zonal.at[0], west_msg.at[pl.ds(4 * K, K)])
    add(diffusivity.at[0], west_msg.at[pl.ds(5 * K, K)])
    fifth = len(copies)
    upper = pltpu.make_async_copy(turbulence.at[:, K - 1, :], level_msg.at[4], sems.at[fifth])
    lower = pltpu.make_async_copy(vertical.at[:, 0, :], level_msg.at[4], sems.at[fifth])

    @pl.when(slab == 0)
    def _():
        upper.start()

    @pl.when(slab == 1)
    def _():
        lower.start()

    depth_rows[...] = (sea[...] * (bottom[...] + 1)).astype(F32)
    last = [
        pltpu.make_async_copy(depth_rows.at[pl.ds(8, 8)], east_msg.at[pl.ds(4 * K, 8)], sems.at[fifth + 1]),
        pltpu.make_async_copy(depth_rows.at[pl.ds(0, 8)], west_msg.at[pl.ds(6 * K, 8)], sems.at[fifth + 2]),
    ]
    for copy in last:
        copy.start()
    upper.wait()
    for copy in copies + last:
        copy.wait()


def interior_kernel(
    tracers, zonal, merid, vertical, diffusivity, turbulence, sea, bottom,
    p_out, inverse_out, carry_out, ratio_out, tail_out, cols, zcols, dcols, own_rows, extra_rows,
    q, zc, mc, vc, df, tb, below_flux, rate, sems, col_sems
):
    slab = lax.axis_index("lev")
    edge = (K - 1) * (1 - slab)
    base = K * slab

    def copies(k):
        pairs = [
            (tracers.at[:, :, k, :], q.at[:, k]),
            (zonal.at[:, k, :], zc.at[k]),
            (merid.at[:, k, :], mc.at[k]),
            (vertical.at[:, k, :], vc.at[k]),
            (diffusivity.at[:, k, :], df.at[k]),
            (turbulence.at[:, k, :], tb.at[k]),
        ]
        return [pltpu.make_async_copy(a, b, sems.at[i, k]) for i, (a, b) in enumerate(pairs)]

    for k in range(AHEAD):
        for copy in copies(k):
            copy.start()

    depth = sea[...] * (bottom[...] + 1)
    depth_west = west_depth(depth)
    row = lax.broadcasted_iota(jnp.int32, (X, Y), 0)
    depth_west_inner = jnp.where((row >= 2) & (row <= X - 2), depth_west, 0)
    depth_south = south_depth(depth)
    column_copies = []

    def add(src, dst):
        column_copies.append(pltpu.make_async_copy(src, dst, col_sems.at[len(column_copies)]))
        column_copies[-1].start()

    for i, x in enumerate((0, 1, 2, X - 3, X - 2, X - 1)):
        for t in range(2):
            add(tracers.at[t, x], cols.at[t, i])
    for i, x in enumerate((0, 1, X - 1)):
        add(zonal.at[x], zcols.at[i])
        add(diffusivity.at[x], dcols.at[i])
    below_flux[...] = jnp.zeros_like(below_flux)
    rate[0] = jnp.zeros((X, Y), F32)

    for k in range(2):
        for copy in copies(k):
            copy.wait()

    def process(k, below):
        ahead = jnp.minimum(k + 2, K - 1)
        level = base + k
        up = jnp.maximum(k - 1, 0)
        down = jnp.minimum(k + 1, K - 1)
        here = [q[t, k] for t in range(2)]
        next_row = [q[t, down] for t in range(2)]
        open_up = jnp.where(k > 0, level, FAR) < depth
        open_down = jnp.where(k < K - 1, level + 1, FAR) < depth
        open_far = jnp.where(k < K - 2, level + 2, FAR) < depth
        grad_up = [jnp.where(open_up, here[t] - q[t, up], 0.0) for t in range(2)]
        grad_down = [jnp.where(open_down, next_row[t] - here[t], 0.0) for t in range(2)]
        grad_far = [jnp.where(open_far, q[t, ahead] - next_row[t], 0.0) for t in range(2)]
        centred = [grad_up[t] + grad_down[t] for t in range(2)]
        known = jnp.where(slab == 0, k < K - 2, k > 0)
        open_flux = jnp.where(known, level + 1, FAR) < depth
        down_courant = jnp.where(open_flux, vc[down], 0.0)
        vert = face_flux(down_courant, here, grad_down, grad_up, grad_far)
        total = []
        for t in range(2):
            total.append(here[t] + below[t] - vert[t])
        rate[k + 1] = jnp.where(level + 1 < depth, tb[k] * lax.rsqrt(tb[k]), 0.0)
        iso_level = jnp.where(k == edge, FAR, level)
        spread = df[k]

        open_west = level < depth_west
        behind = [row_roll(here[t], 1) for t in range(2)]
        grad = [jnp.where(open_west, here[t] - behind[t], 0.0) for t in range(2)]
        flux = face_flux(
            jnp.where(level < depth_west_inner, zc[k], 0.0),
            behind,
            grad,
            [row_roll(grad[t], 1) for t in range(2)],
            [row_roll(grad[t], -1) for t in range(2)],
        )
        iso = isoneutral(
            grad,
            [centred[t] + row_roll(centred[t], 1) for t in range(2)],
            jnp.where(iso_level < depth_west_inner, spread, 0.0),
        )
        for t in range(2):
            net = iso[t] - flux[t]
            total[t] = total[t] + (row_roll(net, -1) - net)

        open_south = level < depth_south
        behind = [lane_roll(here[t], 1) for t in range(2)]
        grad = [jnp.where(open_south, here[t] - behind[t], 0.0) for t in range(2)]
        flux = face_flux(
            jnp.where(open_south, mc[k], 0.0),
            behind,
            grad,
            [lane_roll(grad[t], 1) for t in range(2)],
            [lane_roll(grad[t], -1) for t in range(2)],
        )
        iso = isoneutral(
            grad,
            [centred[t] + lane_roll(centred[t], 1) for t in range(2)],
            jnp.where(iso_level < depth_south, spread, 0.0),
        )
        for t in range(2):
            net = iso[t] - flux[t]
            total[t] = total[t] + (lane_roll(net, -1) - net)
            for lane in range(LANES):
                p_out[t, lane, pl.ds(k * X, X), :] = total[t][:, lane * 128 : lane * 128 + 128]
        return vert

    @pl.loop(0, K // UNROLL)
    def _(i):
        first = i * UNROLL
        for u in range(UNROLL):
            @pl.when(first + u + AHEAD < K)
            def _():
                for copy in copies(first + u + AHEAD):
                    copy.start()

            @pl.when(first + u + 2 < K)
            def _():
                for copy in copies(first + u + 2):
                    copy.wait()

        below = [below_flux[t] for t in range(2)]
        for u in range(UNROLL):
            below = process(first + u, below)
        for t in range(2):
            below_flux[t] = below[t]

    def eliminate(j, tail):
        prev_face = jnp.where(slab == 0, j, K - j)
        next_face = jnp.where(slab == 0, j + 1, K - 1 - j)
        k = jnp.where(slab == 0, j, K - 1 - j)
        prev_rate = rate[prev_face]
        next_rate = rate[next_face]
        rest = 1.0 + prev_rate * tail
        inverse = reciprocal(rest + next_rate)
        inverse_out[k] = inverse
        carry_out[k] = prev_rate * inverse
        ratio_out[k] = next_rate * inverse
        return rest * inverse

    tail_out[0] = lax.fori_loop(0, K - 1, eliminate, jnp.zeros((X, Y), F32))
    tail_out[1] = rate[jnp.where(slab == 0, K - 1, 1)]
    for t in range(2):
        for i in range(3):
            own_rows[t, i] = q[t, (K - 3) * (1 - slab) + i]
    extra_rows[0] = vc[edge]
    extra_rows[1] = vc[1]
    extra_rows[2] = df[edge]
    extra_rows[3] = tb[K - 1]
    for copy in column_copies:
        copy.wait()


def edge_kernel(
    east_msg, west_msg, level_msg, sea, bottom,
    p_in, inverse, carry, tail, cols, zcols, dcols, own_rows, extra_rows,
    v_out, meet_out, corner_out,
    p, rows, sem
):
    slab = lax.axis_index("lev")
    edge = (K - 1) * (1 - slab)
    inner = 30 - 29 * slab
    base = K * slab
    fetch = pltpu.make_async_copy(p_in, p, sem)
    fetch.start()
    for t in range(2):
        for i in range(3):
            rows[t, 2 * slab + i] = own_rows[t, i]
        for i in range(2):
            rows[t, 3 * (1 - slab) + i] = level_msg[2 * t + i]

    depth = sea[...] * (bottom[...] + 1)

    level = base + lax.broadcasted_iota(jnp.int32, (K, Y), 0)
    local_row = lax.broadcasted_iota(jnp.int32, (K, Y), 0)

    def zonal_edge(q, depths, halo, courants, spreads, outer_face):
        centred = []
        for i in range(3):
            column_depth = depths[i + 1]
            pair = []
            for t in range(2):
                mine = q[t][i + 1]
                outer = halo[t][i]
                below = jnp.where(local_row == K - 1, outer, row_roll(mine, -1))
                down = jnp.where(level + 1 < column_depth, below - mine, 0.0)
                top = jnp.where(
                    (slab == 1) & (level < column_depth), mine - outer, 0.0
                )
                up = jnp.where(local_row == 0, top, row_roll(down, 1))
                pair.append(up + down)
            centred.append(pair)
        opened = [level < jnp.minimum(depths[i], depths[i + 1]) for i in range(4)]
        grads = [
            [jnp.where(opened[i], q[t][i + 1] - q[t][i], 0.0) for t in range(2)] for i in range(4)
        ]
        nets = []
        for f in range(2):
            flux = face_flux(
                jnp.where(opened[f + 1], courants[f], 0.0),
                [q[t][f + 1] for t in range(2)],
                grads[f + 1],
                grads[f],
                grads[f + 2],
            )
            iso = isoneutral(
                grads[f + 1],
                [centred[f][t] + centred[f + 1][t] for t in range(2)],
                jnp.where(opened[f + 1] & (local_row != edge) if f == outer_face else opened[f + 1], spreads[f], 0.0),
            )
            nets.append([iso[t] - flux[t] for t in range(2)])
        return nets

    def add_column(t, x, values):
        for lane in range(LANES):
            where = (t, lane, pl.ds(x, K, stride=X), slice(None))
            p[where] = p[where] + values[:, lane * 128 : lane * 128 + 128]

    def depth_row(x):
        return depth[x : x + 1]

    def near(t, x):
        return level_msg[2 * t + slab, x : x + 1, :]

    west_depths = east_msg[4 * K : 4 * K + 8, :].astype(jnp.int32)
    nets = zonal_edge(
        [
            [east_msg[(2 * t + i) * K : (2 * t + i + 1) * K, :] for i in range(2)]
            + [cols[t, i] for i in range(3)]
            for t in range(2)
        ],
        [west_depths[6:7], west_depths[7:8], depth_row(0), depth_row(1), depth_row(2)],
        [[near(t, 0), near(t, 0), near(t, 1)] for t in range(2)],
        [zcols[0], zcols[1]],
        [dcols[0], dcols[1]],
        0,
    )
    fetch.wait()
    for t in range(2):
        add_column(t, 0, nets[1][t] - nets[0][t])
        add_column(t, 1, -nets[1][t])
    east_depths = west_msg[6 * K : 6 * K + 8, :].astype(jnp.int32)
    nets = zonal_edge(
        [
            [cols[t, 3 + i] for i in range(3)]
            + [west_msg[(2 * t + i) * K : (2 * t + i + 1) * K, :] for i in range(2)]
            for t in range(2)
        ],
        [depth_row(X - 3), depth_row(X - 2), depth_row(X - 1), east_depths[0:1], east_depths[1:2]],
        [[near(t, X - 2), near(t, X - 1), near(t, X - 1)] for t in range(2)],
        [zcols[2], west_msg[4 * K : 5 * K, :]],
        [dcols[2], west_msg[5 * K : 6 * K, :]],
        1,
    )
    for t in range(2):
        add_column(t, X - 2, nets[0][t])
        add_column(t, X - 1, nets[1][t] - nets[0][t])

    start = K - 3 + slab
    q = [[rows[t, i] for i in range(5)] for t in range(2)]
    grads = [
        [jnp.where(start + i + 1 < depth, q[t][i + 1] - q[t][i], 0.0) for t in range(2)]
        for i in range(4)
    ]
    other = level_msg[4]
    courant_low = jnp.where(slab == 0, other, extra_rows[1])
    above = face_flux(
        jnp.where(start + 2 < depth, extra_rows[0], 0.0),
        [q[t][1] for t in range(2)], grads[1], grads[0], grads[2],
    )
    under = face_flux(
        jnp.where(start + 3 < depth, courant_low, 0.0),
        [q[t][2] for t in range(2)], grads[2], grads[1], grads[3],
    )
    centred = [grads[1][t] + grads[2][t] for t in range(2)]
    here = [q[t][2] for t in range(2)]
    mid = start + 2
    depth_west = west_depth(depth)
    row = lax.broadcasted_iota(jnp.int32, (X, Y), 0)
    depth_west_inner = jnp.where((row >= 2) & (row <= X - 2), depth_west, 0)
    depth_south = south_depth(depth)
    spread = extra_rows[2]
    grad = [jnp.where(mid < depth_west, here[t] - row_roll(here[t], 1), 0.0) for t in range(2)]
    zonal_iso = isoneutral(
        grad,
        [centred[t] + row_roll(centred[t], 1) for t in range(2)],
        jnp.where(mid < depth_west_inner, spread, 0.0),
    )
    grad = [jnp.where(mid < depth_south, here[t] - lane_roll(here[t], 1), 0.0) for t in range(2)]
    merid_iso = isoneutral(
        grad,
        [centred[t] + lane_roll(centred[t], 1) for t in range(2)],
        jnp.where(mid < depth_south, spread, 0.0),
    )

    def add_level(t, k, values):
        for lane in range(LANES):
            where = (t, lane, pl.ds(pl.multiple_of(k * X, X), X), slice(None))
            p[where] = p[where] + values[:, lane * 128 : lane * 128 + 128]

    for t in range(2):
        change = row_roll(zonal_iso[t], -1) - zonal_iso[t]
        change = change + (lane_roll(merid_iso[t], -1) - merid_iso[t])
        add_level(t, edge, change - (under[t] - above[t]))
        add_level(t, inner, jnp.where(slab == 0, -above[t], under[t]))

    def provisional(t, k):
        rows_at = pl.ds(pl.multiple_of(k * X, X), X)
        return jnp.concatenate([p[t, lane, rows_at, :] for lane in range(LANES)], axis=1)

    def forward(j, values):
        k = jnp.where(slab == 0, j, K - 1 - j)
        inv = inverse[k]
        car = carry[k]
        new = tuple(provisional(t, k) * inv + car * values[t] for t in range(2))
        for t in range(2):
            v_out[t, k] = new[t]
        return new

    zero = jnp.zeros((X, Y), F32)
    values = lax.fori_loop(0, K - 1, forward, (zero, zero))
    meet_rate = jnp.where(K < depth, jnp.sqrt(jnp.where(slab == 0, extra_rows[3], other)), 0.0)
    prev_rate = tail[1]
    rest = 1.0 + prev_rate * tail[0]
    inv = 1.0 / (rest + meet_rate)
    for t in range(2):
        meet_out[t] = (provisional(t, edge) + prev_rate * values[t]) * inv
    meet_out[2] = rest * inv

    corner_out[...] = jnp.zeros_like(corner_out)
    meet_out[3] = jnp.zeros((X, Y), F32)
    own_level = base + edge
    outside = ((east_msg, K, west_depths[7:8], 0), (west_msg, 0, east_depths[0:1], X - 1))
    open_inner = jnp.where(slab == 0, K - 1, K + 1)
    open_other = jnp.where(slab == 0, K + 1, K - 1)
    for side, (msg, offset, outer_depth, x) in enumerate(outside):
        column_depth = depth_row(x)
        for t in range(2):
            at_edge = offset + 2 * t * K + edge
            outer = msg[pl.ds(at_edge, 1), :]
            outer_inner = msg[pl.ds(offset + 2 * t * K + inner, 1), :]
            meet_out[3, 2 * t + side : 2 * t + side + 1, :] = outer
            meet_out[3, 4 + 2 * t + side : 5 + 2 * t + side, :] = jnp.where(
                open_inner < outer_depth, outer - outer_inner, 0.0
            )
            mine = own_rows[t, 2 * (1 - slab), x : x + 1, :]
            mine_inner = own_rows[t, 1, x : x + 1, :]
            theirs = near(t, x)
            theirs_inner = level_msg[2 * t + 1 - slab, x : x + 1, :]
            cross = jnp.where(K < column_depth, theirs - mine, 0.0)
            corner_out[t, side : side + 1, :] = mine
            corner_out[t, 2 + side : 3 + side, :] = theirs
            corner_out[2 + t, side : side + 1, :] = cross + jnp.where(
                open_inner < column_depth, mine - mine_inner, 0.0
            )
            corner_out[2 + t, 2 + side : 3 + side, :] = (
                jnp.where(open_other < column_depth, theirs - theirs_inner, 0.0) - cross
            )
        spread_row = dcols[0, pl.ds(edge, 1), :] if side == 0 else west_msg[pl.ds(5 * K + edge, 1), :]
        meet_out[3, 8 + side : 9 + side, :] = jnp.where(
            own_level < jnp.minimum(outer_depth, column_depth), spread_row, 0.0
        )
        meet_out[3, 10 + side : 11 + side, :] = inv[x : x + 1]
        shared = jnp.where(K < outer_depth, 1.0, 0.0)
        corner_out[4, side : side + 1, :] = shared
        corner_out[4, 2 + side : 3 + side, :] = shared


def finish_kernel(v, ratio, mine, theirs, corner, out, u, gathered, change, sems):
    slab = lax.axis_index("lev")
    for i in range(6):
        gathered[i, 0:2, :] = mine[3, 2 * i : 2 * i + 2, :]
        gathered[i, 2:4, :] = theirs[3, 2 * i : 2 * i + 2, :]
        gathered[i, 4:6, :] = theirs[3, 2 * i : 2 * i + 2, :]
        gathered[i, 6:8, :] = mine[3, 2 * i : 2 * i + 2, :]
    grad = []
    vert = []
    for t in range(2):
        outer = gathered[t]
        other = row_roll(outer, 4)
        grad.append(outer - corner[t])
        vert.append(corner[2 + t] + gathered[2 + t] + corner[4] * (other - outer))
    flux = isoneutral(grad, vert, gathered[4])
    change[...] = jnp.zeros_like(change)
    for t in range(2):
        moved = flux[t] * gathered[5]
        for i in range(2):
            change[i, t, 0:1, :] = moved[2 * i : 2 * i + 1]
            change[i, t, X - 1 : X, :] = moved[2 * i + 1 : 2 * i + 2]
    own_tail = mine[2]
    own_ratio = 1.0 - own_tail
    scale = reciprocal(own_tail + own_ratio * theirs[2])
    last = tuple(
        (mine[t] + change[0, t] + own_ratio * (theirs[t] + change[1, t])) * scale for t in range(2)
    )
    edge = (K - 1) * (1 - slab)

    def copies(k):
        return [pltpu.make_async_copy(u.at[t, k], out.at[t, :, k, :], sems.at[t, k]) for t in range(2)]

    for t in range(2):
        u[t, edge] = last[t]
    for copy in copies(edge):
        copy.start()

    def backward(i, values):
        j = K - 2 - i
        k = jnp.where(slab == 0, j, K - 1 - j)
        rat = ratio[k]
        new = tuple(v[t, k] + rat * values[t] for t in range(2))
        for t in range(2):
            u[t, k] = new[t]
        for copy in copies(k):
            copy.start()
        return new

    lax.fori_loop(0, K - 1, backward, last)

    @pl.loop(0, K)
    def _(k):
        for copy in copies(k):
            copy.wait()


def shape(*dims):
    return jax.ShapeDtypeStruct(dims, F32)


def params(mib):
    return pltpu.CompilerParams(vmem_limit_bytes=mib * 1024 * 1024)


def local(
    tracers, zonal, merid, vertical, diffusivity, turbulence, sea, bottom
):
    count = lax.axis_size("tile")
    east_msg, west_msg, level_msg = pl.pallas_call(
        pack_kernel,
        name="pack",
        in_specs=[any_spec()] * 5 + [vmem_spec()] * 2,
        out_specs=[vmem_spec()] * 3,
        out_shape=[shape(4 * K + 8, Y), shape(6 * K + 8, Y), shape(5, X, Y)],
        scratch_shapes=[pltpu.VMEM((X, Y), F32), pltpu.SemaphoreType.DMA((24,))],
        compiler_params=params(60),
    )(tracers, zonal, vertical, diffusivity, turbulence, sea, bottom)

    eastward = [(i, (i + 1) % count) for i in range(count)]
    east_in = lax.ppermute(east_msg, "tile", eastward)
    west_in = lax.ppermute(west_msg, "tile", [(b, a) for a, b in eastward])
    level_in = lax.ppermute(level_msg, "lev", [(0, 1), (1, 0)])

    p, inverse, carry, ratio, tail, *pieces = pl.pallas_call(
        interior_kernel,
        name="interior",
        in_specs=[any_spec()] * 6 + [vmem_spec()] * 2,
        out_specs=[vmem_spec()] * 10,
        out_shape=[
            shape(2, LANES, K * X, 128), shape(K, X, Y), shape(K, X, Y), shape(K, X, Y), shape(2, X, Y),
            shape(2, 6, K, Y), shape(3, K, Y), shape(3, K, Y), shape(2, 3, X, Y), shape(4, X, Y),
        ],
        scratch_shapes=[
            pltpu.VMEM((2, K, X, Y), F32),
            pltpu.VMEM((K, X, Y), F32),
            pltpu.VMEM((K, X, Y), F32),
            pltpu.VMEM((K, X, Y), F32),
            pltpu.VMEM((K, X, Y), F32),
            pltpu.VMEM((K, X, Y), F32),
            pltpu.VMEM((2, X, Y), F32),
            pltpu.VMEM((K + 1, X, Y), F32),
            pltpu.SemaphoreType.DMA((6, K)),
            pltpu.SemaphoreType.DMA((18,)),
        ],
        compiler_params=params(50),
        cost_estimate=pl.CostEstimate(flops=50_000_000, bytes_accessed=40_000_000, transcendentals=0),
    )(tracers, zonal, merid, vertical, diffusivity, turbulence, sea, bottom)

    v, meet, corner = pl.pallas_call(
        edge_kernel,
        name="edges",
        in_specs=[vmem_spec()] * 5 + [any_spec()] + [vmem_spec()] * 8,
        out_specs=[vmem_spec()] * 3,
        out_shape=[shape(2, K, X, Y), shape(4, X, Y), shape(5, 8, Y)],
        scratch_shapes=[
            pltpu.VMEM((2, LANES, K * X, 128), F32),
            pltpu.VMEM((2, 5, X, Y), F32),
            pltpu.SemaphoreType.DMA,
        ],
        compiler_params=params(50),
    )(east_in, west_in, level_in, sea, bottom, p, inverse, carry, tail, *pieces)

    meet_in = lax.ppermute(meet, "lev", [(0, 1), (1, 0)])
    return pl.pallas_call(
        finish_kernel,
        name="finish",
        in_specs=[vmem_spec()] * 5,
        out_specs=any_spec(),
        out_shape=shape(2, X, K, Y),
        scratch_shapes=[
            pltpu.VMEM((2, K, X, Y), F32),
            pltpu.VMEM((6, 8, Y), F32),
            pltpu.VMEM((2, 2, X, Y), F32),
            pltpu.SemaphoreType.DMA((2, K)),
        ],
        compiler_params=params(50),
    )(v, ratio, meet, meet_in, corner)


def solution(mesh):
    return jax.shard_map(
        local,
        mesh=mesh,
        in_specs=(
            P(None, "tile", "lev", None),
            P("tile", "lev", None),
            P("tile", "lev", None),
            P("tile", "lev", None),
            P("tile", "lev", None),
            P("tile", "lev", None),
            P("tile", None),
            P("tile", None),
        ),
        out_specs=P(None, "tile", "lev", None),
        check_vma=False,
    )
```

```python
import jax
import jax.numpy as jnp
from jax import lax
from jax.experimental import pallas as pl
from jax.experimental.pallas import tpu as pltpu
from jax.sharding import PartitionSpec as P

thermal_coef = 0.2
haline_coef = 0.8
taper_eps = 0.05

X = 16
K = 32
Y = 384
LANES = 3
UNROLL = 2
AHEAD = 8
FAR = 1 << 20
F32 = jnp.float32


def any_spec():
    return pl.BlockSpec(memory_space=pl.ANY)


def vmem_spec():
    return pl.BlockSpec(memory_space=pltpu.VMEM)


def face_flux(courant, behind, grad, back, front):
    half = 0.5 * courant
    half_speed = jnp.abs(half)
    weight = half_speed - 2.0 * half_speed * half_speed
    lag = half - half_speed
    forward = courant > 0.0
    fluxes = []
    for t in range(2):
        upwind = jnp.where(forward, back[t], front[t])
        low = jnp.minimum(grad[t], 0.0)
        high = jnp.maximum(grad[t], 0.0)
        double = jnp.minimum(jnp.maximum(upwind + upwind, low), high)
        excess = jnp.minimum(jnp.maximum(upwind - grad[t], low), high)
        fluxes.append(courant * behind[t] + lag * grad[t] + weight * (double + excess))
    return fluxes


def reciprocal(values):
    guess = pl.reciprocal(values, approx=True)
    return guess * (2.0 - values * guess)


def isoneutral(grad, vert, coeff):
    ratio = haline_coef / thermal_coef
    dens_side = ratio * grad[1] - grad[0]
    dens_vert = ratio * vert[1] - vert[0]
    floor = 16.0 * taper_eps / (thermal_coef * thermal_coef)
    slope = dens_side * dens_vert * reciprocal(dens_vert * dens_vert + floor)
    return [coeff * (grad[t] - slope * vert[t]) for t in range(2)]


def lane_roll(values, shift):
    return pltpu.roll(values, shift % Y, 1)


def row_roll(values, shift):
    return pltpu.roll(values, shift % values.shape[0], 0)


def south_depth(depth):
    lane = lax.broadcasted_iota(jnp.int32, depth.shape, 1)
    return jnp.where(lane == 0, 0, jnp.minimum(depth, lane_roll(depth, 1)))


def west_depth(depth):
    return jnp.minimum(depth, row_roll(depth, 1))


def pack_kernel(
    tracers, zonal, vertical, diffusivity, turbulence, sea, bottom,
    east_msg, west_msg, level_msg, depth_rows, sems
):
    slab = lax.axis_index("lev")
    first = (K - 2) * (1 - slab)
    copies = []

    def add(src, dst):
        copies.append(pltpu.make_async_copy(src, dst, sems.at[len(copies)]))
        copies[-1].start()

    for t in range(2):
        for i in range(2):
            rows = pl.ds((2 * t + i) * K, K)
            add(tracers.at[t, X - 2 + i], east_msg.at[rows])
            add(tracers.at[t, i], west_msg.at[rows])
            add(tracers.at[t, :, first + i, :], level_msg.at[2 * t + i])
    add(zonal.at[0], west_msg.at[pl.ds(4 * K, K)])
    add(diffusivity.at[0], west_msg.at[pl.ds(5 * K, K)])
    fifth = len(copies)
    upper = pltpu.make_async_copy(turbulence.at[:, K - 1, :], level_msg.at[4], sems.at[fifth])
    lower = pltpu.make_async_copy(vertical.at[:, 0, :], level_msg.at[4], sems.at[fifth])

    @pl.when(slab == 0)
    def _():
        upper.start()

    @pl.when(slab == 1)
    def _():
        lower.start()

    depth_rows[...] = (sea[...] * (bottom[...] + 1)).astype(F32)
    last = [
        pltpu.make_async_copy(depth_rows.at[pl.ds(8, 8)], east_msg.at[pl.ds(4 * K, 8)], sems.at[fifth + 1]),
        pltpu.make_async_copy(depth_rows.at[pl.ds(0, 8)], west_msg.at[pl.ds(6 * K, 8)], sems.at[fifth + 2]),
    ]
    for copy in last:
        copy.start()
    upper.wait()
    for copy in copies + last:
        copy.wait()


def interior_kernel(
    tracers, zonal, merid, vertical, diffusivity, turbulence, sea, bottom,
    p_first, p_second, inverse_out, carry_out, ratio_out, tail_out, cols, zcols, dcols, own_rows, extra_rows,
    q, zc, mc, vc, df, tb, below_flux, grads_kept, sems, col_sems
):
    slab = lax.axis_index("lev")
    edge = (K - 1) * (1 - slab)
    base = K * slab

    def copies(k):
        pairs = [
            (tracers.at[:, :, k, :], q.at[:, k]),
            (zonal.at[:, k, :], zc.at[k]),
            (merid.at[:, k, :], mc.at[k]),
            (vertical.at[:, k, :], vc.at[k]),
            (diffusivity.at[:, k, :], df.at[k]),
            (turbulence.at[:, jnp.where(slab == 0, k, jnp.maximum(K - 2 - k, 0)), :], tb.at[k]),
        ]
        return [pltpu.make_async_copy(a, b, sems.at[i, k]) for i, (a, b) in enumerate(pairs)]

    for k in range(AHEAD):
        for copy in copies(k):
            copy.start()

    depth = sea[...] * (bottom[...] + 1)
    depth_west = west_depth(depth)
    row = lax.broadcasted_iota(jnp.int32, (X, Y), 0)
    depth_west_inner = jnp.where((row >= 2) & (row <= X - 2), depth_west, 0)
    depth_south = south_depth(depth)
    column_copies = []

    def add(src, dst):
        column_copies.append(pltpu.make_async_copy(src, dst, col_sems.at[len(column_copies)]))
        column_copies[-1].start()

    for i, x in enumerate((0, 1, 2, X - 3, X - 2, X - 1)):
        for t in range(2):
            add(tracers.at[t, x], cols.at[t, i])
    for i, x in enumerate((0, 1, X - 1)):
        add(zonal.at[x], zcols.at[i])
        add(diffusivity.at[x], dcols.at[i])
    below_flux[...] = jnp.zeros_like(below_flux)
    tail_out[...] = jnp.zeros_like(tail_out)
    grads_kept[0] = jnp.zeros((2, X, Y), F32)

    for k in range(2):
        for copy in copies(k):
            copy.wait()
    for t in range(2):
        grads_kept[1, t] = jnp.where(base + 1 < depth, q[t, 1] - q[t, 0], 0.0)

    def eliminate(j, tail, prev_rate):
        face = jnp.where(slab == 0, j + 1, 2 * K - 1 - j)
        turb = tb[j]
        next_rate = jnp.where(face < depth, turb * lax.rsqrt(turb), 0.0)
        rest = 1.0 + prev_rate * tail
        inverse = reciprocal(rest + next_rate)
        inverse_out[j] = inverse
        carry_out[j] = prev_rate * inverse
        ratio_out[j] = next_rate * inverse
        return rest * inverse, next_rate

    def process(k, below, grad_up, grad_down):
        ahead = jnp.minimum(k + 2, K - 1)
        level = base + k
        down = jnp.minimum(k + 1, K - 1)
        here = [q[t, k] for t in range(2)]
        next_row = [q[t, down] for t in range(2)]
        open_far = jnp.where(k < K - 2, level + 2, FAR) < depth
        grad_far = [jnp.where(open_far, q[t, ahead] - next_row[t], 0.0) for t in range(2)]
        centred = [grad_up[t] + grad_down[t] for t in range(2)]
        known = jnp.where(slab == 0, k < K - 2, k > 0)
        open_flux = jnp.where(known, level + 1, FAR) < depth
        down_courant = jnp.where(open_flux, vc[down], 0.0)
        vert = face_flux(down_courant, here, grad_down, grad_up, grad_far)
        total = []
        for t in range(2):
            total.append(here[t] + below[t] - vert[t])
        iso_level = jnp.where(k == edge, FAR, level)
        spread = df[k]

        open_west = level < depth_west
        behind = [row_roll(here[t], 1) for t in range(2)]
        grad = [jnp.where(open_west, here[t] - behind[t], 0.0) for t in range(2)]
        flux = face_flux(
            jnp.where(level < depth_west_inner, zc[k], 0.0),
            behind,
            grad,
            [row_roll(grad[t], 1) for t in range(2)],
            [row_roll(grad[t], -1) for t in range(2)],
        )
        iso = isoneutral(
            grad,
            [centred[t] + row_roll(centred[t], 1) for t in range(2)],
            jnp.where(iso_level < depth_west_inner, spread, 0.0),
        )
        for t in range(2):
            net = iso[t] - flux[t]
            total[t] = total[t] + (row_roll(net, -1) - net)

        open_south = level < depth_south
        behind = [lane_roll(here[t], 1) for t in range(2)]
        grad = [jnp.where(open_south, here[t] - behind[t], 0.0) for t in range(2)]
        flux = face_flux(
            jnp.where(open_south, mc[k], 0.0),
            behind,
            grad,
            [lane_roll(grad[t], 1) for t in range(2)],
            [lane_roll(grad[t], -1) for t in range(2)],
        )
        iso = isoneutral(
            grad,
            [centred[t] + lane_roll(centred[t], 1) for t in range(2)],
            jnp.where(iso_level < depth_south, spread, 0.0),
        )
        for t in range(2):
            net = iso[t] - flux[t]
            total[t] = total[t] + (lane_roll(net, -1) - net)
            for lane in range(LANES):
                (p_first, p_second)[t][lane, pl.ds(k * X, X), :] = total[t][:, lane * 128 : lane * 128 + 128]
        return vert, grad_down, grad_far

    def step(i, start, wait):
        first = i * UNROLL
        for u in range(UNROLL):
            if start:
                for copy in copies(first + u + AHEAD):
                    copy.start()
            if wait:
                for copy in copies(first + u + 2):
                    copy.wait()
        below = [below_flux[t] for t in range(2)]
        grads = [[grads_kept[f, t] for t in range(2)] for f in range(2)]
        tail, prev_rate = tail_out[0], tail_out[1]
        for u in range(UNROLL):
            below, grad_down, grad_far = process(first + u, below, grads[0], grads[1])
            grads = [grad_down, grad_far]
            if wait or u < UNROLL - 1:
                tail, prev_rate = eliminate(first + u, tail, prev_rate)
        for t in range(2):
            below_flux[t] = below[t]
            for f in range(2):
                grads_kept[f, t] = grads[f][t]
        tail_out[0] = tail
        tail_out[1] = prev_rate

    steps = K // UNROLL
    fed = (K - AHEAD) // UNROLL

    @pl.loop(0, fed)
    def _(i):
        step(i, True, True)

    @pl.loop(fed, steps - 1)
    def _(i):
        step(i, False, True)

    step(steps - 1, False, False)
    for t in range(2):
        for i in range(3):
            own_rows[t, i] = q[t, (K - 3) * (1 - slab) + i]
    extra_rows[0] = vc[edge]
    extra_rows[1] = vc[1]
    extra_rows[2] = df[edge]
    extra_rows[3] = tb[K - 1]
    for copy in column_copies:
        copy.wait()


def edge_kernel(
    east_msg, west_msg, level_msg, sea, bottom,
    p_first, p_second, inverse, carry, tail, cols, zcols, dcols, own_rows, extra_rows,
    v_first, v_second, meet_out, corner_out,
    p, rows, sems
):
    slab = lax.axis_index("lev")
    edge = (K - 1) * (1 - slab)
    inner = 30 - 29 * slab
    base = K * slab
    fetches = [
        pltpu.make_async_copy(ref, p.at[t], sems.at[t]) for t, ref in enumerate((p_first, p_second))
    ]
    for fetch in fetches:
        fetch.start()
    for t in range(2):
        for i in range(3):
            rows[t, 2 * slab + i] = own_rows[t, i]
        for i in range(2):
            rows[t, 3 * (1 - slab) + i] = level_msg[2 * t + i]

    depth = sea[...] * (bottom[...] + 1)

    level = base + lax.broadcasted_iota(jnp.int32, (K, Y), 0)
    local_row = lax.broadcasted_iota(jnp.int32, (K, Y), 0)

    def zonal_edge(q, depths, halo, courants, spreads, outer_face):
        centred = []
        for i in range(3):
            column_depth = depths[i + 1]
            pair = []
            for t in range(2):
                mine = q[t][i + 1]
                outer = halo[t][i]
                below = jnp.where(local_row == K - 1, outer, row_roll(mine, -1))
                down = jnp.where(level + 1 < column_depth, below - mine, 0.0)
                top = jnp.where(
                    (slab == 1) & (level < column_depth), mine - outer, 0.0
                )
                up = jnp.where(local_row == 0, top, row_roll(down, 1))
                pair.append(up + down)
            centred.append(pair)
        opened = [level < jnp.minimum(depths[i], depths[i + 1]) for i in range(4)]
        grads = [
            [jnp.where(opened[i], q[t][i + 1] - q[t][i], 0.0) for t in range(2)] for i in range(4)
        ]
        nets = []
        for f in range(2):
            flux = face_flux(
                jnp.where(opened[f + 1], courants[f], 0.0),
                [q[t][f + 1] for t in range(2)],
                grads[f + 1],
                grads[f],
                grads[f + 2],
            )
            iso = isoneutral(
                grads[f + 1],
                [centred[f][t] + centred[f + 1][t] for t in range(2)],
                jnp.where(opened[f + 1] & (local_row != edge) if f == outer_face else opened[f + 1], spreads[f], 0.0),
            )
            nets.append([iso[t] - flux[t] for t in range(2)])
        return nets

    def add_column(t, x, values):
        for lane in range(LANES):
            where = (t, lane, pl.ds(x, K, stride=X), slice(None))
            p[where] = p[where] + values[:, lane * 128 : lane * 128 + 128]

    def depth_row(x):
        return depth[x : x + 1]

    def near(t, x):
        return level_msg[2 * t + slab, x : x + 1, :]

    west_depths = east_msg[4 * K : 4 * K + 8, :].astype(jnp.int32)
    nets = zonal_edge(
        [
            [east_msg[(2 * t + i) * K : (2 * t + i + 1) * K, :] for i in range(2)]
            + [cols[t, i] for i in range(3)]
            for t in range(2)
        ],
        [west_depths[6:7], west_depths[7:8], depth_row(0), depth_row(1), depth_row(2)],
        [[near(t, 0), near(t, 0), near(t, 1)] for t in range(2)],
        [zcols[0], zcols[1]],
        [dcols[0], dcols[1]],
        0,
    )
    for fetch in fetches:
        fetch.wait()
    for t in range(2):
        add_column(t, 0, nets[1][t] - nets[0][t])
        add_column(t, 1, -nets[1][t])
    east_depths = west_msg[6 * K : 6 * K + 8, :].astype(jnp.int32)
    nets = zonal_edge(
        [
            [cols[t, 3 + i] for i in range(3)]
            + [west_msg[(2 * t + i) * K : (2 * t + i + 1) * K, :] for i in range(2)]
            for t in range(2)
        ],
        [depth_row(X - 3), depth_row(X - 2), depth_row(X - 1), east_depths[0:1], east_depths[1:2]],
        [[near(t, X - 2), near(t, X - 1), near(t, X - 1)] for t in range(2)],
        [zcols[2], west_msg[4 * K : 5 * K, :]],
        [dcols[2], west_msg[5 * K : 6 * K, :]],
        1,
    )
    for t in range(2):
        add_column(t, X - 2, nets[0][t])
        add_column(t, X - 1, nets[1][t] - nets[0][t])

    start = K - 3 + slab
    q = [[rows[t, i] for i in range(5)] for t in range(2)]
    grads = [
        [jnp.where(start + i + 1 < depth, q[t][i + 1] - q[t][i], 0.0) for t in range(2)]
        for i in range(4)
    ]
    other = level_msg[4]
    courant_low = jnp.where(slab == 0, other, extra_rows[1])
    above = face_flux(
        jnp.where(start + 2 < depth, extra_rows[0], 0.0),
        [q[t][1] for t in range(2)], grads[1], grads[0], grads[2],
    )
    under = face_flux(
        jnp.where(start + 3 < depth, courant_low, 0.0),
        [q[t][2] for t in range(2)], grads[2], grads[1], grads[3],
    )
    centred = [grads[1][t] + grads[2][t] for t in range(2)]
    here = [q[t][2] for t in range(2)]
    mid = start + 2
    depth_west = west_depth(depth)
    row = lax.broadcasted_iota(jnp.int32, (X, Y), 0)
    depth_west_inner = jnp.where((row >= 2) & (row <= X - 2), depth_west, 0)
    depth_south = south_depth(depth)
    spread = extra_rows[2]
    grad = [jnp.where(mid < depth_west, here[t] - row_roll(here[t], 1), 0.0) for t in range(2)]
    zonal_iso = isoneutral(
        grad,
        [centred[t] + row_roll(centred[t], 1) for t in range(2)],
        jnp.where(mid < depth_west_inner, spread, 0.0),
    )
    grad = [jnp.where(mid < depth_south, here[t] - lane_roll(here[t], 1), 0.0) for t in range(2)]
    merid_iso = isoneutral(
        grad,
        [centred[t] + lane_roll(centred[t], 1) for t in range(2)],
        jnp.where(mid < depth_south, spread, 0.0),
    )

    def add_level(t, k, values):
        for lane in range(LANES):
            where = (t, lane, pl.ds(pl.multiple_of(k * X, X), X), slice(None))
            p[where] = p[where] + values[:, lane * 128 : lane * 128 + 128]

    for t in range(2):
        change = row_roll(zonal_iso[t], -1) - zonal_iso[t]
        change = change + (lane_roll(merid_iso[t], -1) - merid_iso[t])
        add_level(t, edge, change - (under[t] - above[t]))
        add_level(t, inner, jnp.where(slab == 0, -above[t], under[t]))

    def provisional(t, k):
        rows_at = pl.ds(pl.multiple_of(k * X, X), X)
        return jnp.concatenate([p[t, lane, rows_at, :] for lane in range(LANES)], axis=1)

    def forward(j, values):
        k = jnp.where(slab == 0, j, K - 1 - j)
        inv = inverse[j]
        car = carry[j]
        new = tuple(provisional(t, k) * inv + car * values[t] for t in range(2))
        for t in range(2):
            (v_first, v_second)[t][k] = new[t]
        return new

    zero = jnp.zeros((X, Y), F32)
    values = lax.fori_loop(0, K - 1, forward, (zero, zero))
    meet_rate = jnp.where(K < depth, jnp.sqrt(jnp.where(slab == 0, extra_rows[3], other)), 0.0)
    prev_rate = tail[1]
    rest = 1.0 + prev_rate * tail[0]
    inv = 1.0 / (rest + meet_rate)
    for t in range(2):
        meet_out[t] = (provisional(t, edge) + prev_rate * values[t]) * inv
    meet_out[2] = rest * inv

    corner_out[...] = jnp.zeros_like(corner_out)
    meet_out[3] = jnp.zeros((X, Y), F32)
    own_level = base + edge
    outside = ((east_msg, K, west_depths[7:8], 0), (west_msg, 0, east_depths[0:1], X - 1))
    open_inner = jnp.where(slab == 0, K - 1, K + 1)
    open_other = jnp.where(slab == 0, K + 1, K - 1)
    for side, (msg, offset, outer_depth, x) in enumerate(outside):
        column_depth = depth_row(x)
        for t in range(2):
            at_edge = offset + 2 * t * K + edge
            outer = msg[pl.ds(at_edge, 1), :]
            outer_inner = msg[pl.ds(offset + 2 * t * K + inner, 1), :]
            meet_out[3, 2 * t + side : 2 * t + side + 1, :] = outer
            meet_out[3, 4 + 2 * t + side : 5 + 2 * t + side, :] = jnp.where(
                open_inner < outer_depth, outer - outer_inner, 0.0
            )
            mine = own_rows[t, 2 * (1 - slab), x : x + 1, :]
            mine_inner = own_rows[t, 1, x : x + 1, :]
            theirs = near(t, x)
            theirs_inner = level_msg[2 * t + 1 - slab, x : x + 1, :]
            cross = jnp.where(K < column_depth, theirs - mine, 0.0)
            corner_out[t, side : side + 1, :] = mine
            corner_out[t, 2 + side : 3 + side, :] = theirs
            corner_out[2 + t, side : side + 1, :] = cross + jnp.where(
                open_inner < column_depth, mine - mine_inner, 0.0
            )
            corner_out[2 + t, 2 + side : 3 + side, :] = (
                jnp.where(open_other < column_depth, theirs - theirs_inner, 0.0) - cross
            )
        spread_row = dcols[0, pl.ds(edge, 1), :] if side == 0 else west_msg[pl.ds(5 * K + edge, 1), :]
        meet_out[3, 8 + side : 9 + side, :] = jnp.where(
            own_level < jnp.minimum(outer_depth, column_depth), spread_row, 0.0
        )
        meet_out[3, 10 + side : 11 + side, :] = inv[x : x + 1]
        shared = jnp.where(K < outer_depth, 1.0, 0.0)
        corner_out[4, side : side + 1, :] = shared
        corner_out[4, 2 + side : 3 + side, :] = shared


def finish_kernel(v_first, v_second, ratio, mine, theirs, corner, out, u, gathered, change, sems):
    slab = lax.axis_index("lev")
    for i in range(6):
        gathered[i, 0:2, :] = mine[3, 2 * i : 2 * i + 2, :]
        gathered[i, 2:4, :] = theirs[3, 2 * i : 2 * i + 2, :]
        gathered[i, 4:6, :] = theirs[3, 2 * i : 2 * i + 2, :]
        gathered[i, 6:8, :] = mine[3, 2 * i : 2 * i + 2, :]
    grad = []
    vert = []
    for t in range(2):
        outer = gathered[t]
        other = row_roll(outer, 4)
        grad.append(outer - corner[t])
        vert.append(corner[2 + t] + gathered[2 + t] + corner[4] * (other - outer))
    flux = isoneutral(grad, vert, gathered[4])
    change[...] = jnp.zeros_like(change)
    for t in range(2):
        moved = flux[t] * gathered[5]
        for i in range(2):
            change[i, t, 0:1, :] = moved[2 * i : 2 * i + 1]
            change[i, t, X - 1 : X, :] = moved[2 * i + 1 : 2 * i + 2]
    own_tail = mine[2]
    own_ratio = 1.0 - own_tail
    scale = reciprocal(own_tail + own_ratio * theirs[2])
    last = tuple(
        (mine[t] + change[0, t] + own_ratio * (theirs[t] + change[1, t])) * scale for t in range(2)
    )
    edge = (K - 1) * (1 - slab)

    def copies(k):
        return [pltpu.make_async_copy(u.at[t, k], out.at[t, :, k, :], sems.at[t, k]) for t in range(2)]

    for t in range(2):
        u[t, edge] = last[t]
    for copy in copies(edge):
        copy.start()

    def backward(i, values):
        j = K - 2 - i
        k = jnp.where(slab == 0, j, K - 1 - j)
        rat = ratio[j]
        new = tuple(v[k] + rat * values[t] for t, v in enumerate((v_first, v_second)))
        for t in range(2):
            u[t, k] = new[t]
        for copy in copies(k):
            copy.start()
        return new

    lax.fori_loop(0, K - 1, backward, last)

    @pl.loop(0, K)
    def _(k):
        for copy in copies(k):
            copy.wait()


def shape(*dims):
    return jax.ShapeDtypeStruct(dims, F32)


def params(mib):
    return pltpu.CompilerParams(vmem_limit_bytes=mib * 1024 * 1024)


def local(
    tracers, zonal, merid, vertical, diffusivity, turbulence, sea, bottom
):
    count = lax.axis_size("tile")
    east_msg, west_msg, level_msg = pl.pallas_call(
        pack_kernel,
        name="pack",
        in_specs=[any_spec()] * 5 + [vmem_spec()] * 2,
        out_specs=[vmem_spec()] * 3,
        out_shape=[shape(4 * K + 8, Y), shape(6 * K + 8, Y), shape(5, X, Y)],
        scratch_shapes=[pltpu.VMEM((X, Y), F32), pltpu.SemaphoreType.DMA((24,))],
        compiler_params=params(60),
    )(tracers, zonal, vertical, diffusivity, turbulence, sea, bottom)

    eastward = [(i, (i + 1) % count) for i in range(count)]
    east_in = lax.ppermute(east_msg, "tile", eastward)
    west_in = lax.ppermute(west_msg, "tile", [(b, a) for a, b in eastward])
    level_in = lax.ppermute(level_msg, "lev", [(0, 1), (1, 0)])

    p_first, p_second, inverse, carry, ratio, tail, *pieces = pl.pallas_call(
        interior_kernel,
        name="interior",
        in_specs=[any_spec()] * 6 + [vmem_spec()] * 2,
        out_specs=[vmem_spec()] * 11,
        out_shape=[
            shape(LANES, K * X, 128), shape(LANES, K * X, 128), shape(K, X, Y), shape(K, X, Y), shape(K, X, Y),
            shape(2, X, Y),
            shape(2, 6, K, Y), shape(3, K, Y), shape(3, K, Y), shape(2, 3, X, Y), shape(4, X, Y),
        ],
        scratch_shapes=[
            pltpu.VMEM((2, K, X, Y), F32),
            pltpu.VMEM((K, X, Y), F32),
            pltpu.VMEM((K, X, Y), F32),
            pltpu.VMEM((K, X, Y), F32),
            pltpu.VMEM((K, X, Y), F32),
            pltpu.VMEM((K, X, Y), F32),
            pltpu.VMEM((2, X, Y), F32),
            pltpu.VMEM((2, 2, X, Y), F32),
            pltpu.SemaphoreType.DMA((6, K)),
            pltpu.SemaphoreType.DMA((18,)),
        ],
        compiler_params=params(48),
        cost_estimate=pl.CostEstimate(flops=50_000_000, bytes_accessed=40_000_000, transcendentals=0),
    )(tracers, zonal, merid, vertical, diffusivity, turbulence, sea, bottom)

    v_first, v_second, meet, corner = pl.pallas_call(
        edge_kernel,
        name="edges",
        in_specs=[vmem_spec()] * 15,
        out_specs=[vmem_spec()] * 4,
        out_shape=[shape(K, X, Y), shape(K, X, Y), shape(4, X, Y), shape(5, 8, Y)],
        scratch_shapes=[
            pltpu.VMEM((2, LANES, K * X, 128), F32),
            pltpu.VMEM((2, 5, X, Y), F32),
            pltpu.SemaphoreType.DMA((2,)),
        ],
        compiler_params=params(46),
    )(east_in, west_in, level_in, sea, bottom, p_first, p_second, inverse, carry, tail, *pieces)

    meet_in = lax.ppermute(meet, "lev", [(0, 1), (1, 0)])
    return pl.pallas_call(
        finish_kernel,
        name="finish",
        in_specs=[vmem_spec()] * 6,
        out_specs=any_spec(),
        out_shape=shape(2, X, K, Y),
        scratch_shapes=[
            pltpu.VMEM((2, K, X, Y), F32),
            pltpu.VMEM((6, 8, Y), F32),
            pltpu.VMEM((2, 2, X, Y), F32),
            pltpu.SemaphoreType.DMA((2, K)),
        ],
        compiler_params=params(46),
    )(v_first, v_second, ratio, meet, meet_in, corner)


def solution(mesh):
    return jax.shard_map(
        local,
        mesh=mesh,
        in_specs=(
            P(None, "tile", "lev", None),
            P("tile", "lev", None),
            P("tile", "lev", None),
            P("tile", "lev", None),
            P("tile", "lev", None),
            P("tile", "lev", None),
            P("tile", None),
            P("tile", None),
        ),
        out_specs=P(None, "tile", "lev", None),
        check_vma=False,
    )
```

```python
import jax
import jax.numpy as jnp
from jax import lax
from jax.experimental import pallas as pl
from jax.experimental.pallas import tpu as pltpu
from jax.sharding import PartitionSpec as P

thermal_coef = 0.2
haline_coef = 0.8
taper_eps = 0.05

X = 16
K = 32
Y = 384
LANES = 3
UNROLL = 2
AHEAD = 8
FAR = 1 << 20
F32 = jnp.float32


def any_spec():
    return pl.BlockSpec(memory_space=pl.ANY)


def vmem_spec():
    return pl.BlockSpec(memory_space=pltpu.VMEM)


def face_flux(courant, behind, grad, back, front):
    half = 0.5 * courant
    half_speed = jnp.abs(half)
    weight = half_speed - 2.0 * half_speed * half_speed
    lag = half - half_speed
    forward = courant > 0.0
    fluxes = []
    for t in range(2):
        upwind = jnp.where(forward, back[t], front[t])
        low = jnp.minimum(grad[t], 0.0)
        high = jnp.maximum(grad[t], 0.0)
        double = jnp.minimum(jnp.maximum(upwind + upwind, low), high)
        excess = jnp.minimum(jnp.maximum(upwind - grad[t], low), high)
        fluxes.append(courant * behind[t] + lag * grad[t] + weight * (double + excess))
    return fluxes


def reciprocal(values):
    guess = pl.reciprocal(values, approx=True)
    return guess * (2.0 - values * guess)


def isoneutral(grad, vert, coeff):
    ratio = haline_coef / thermal_coef
    dens_side = ratio * grad[1] - grad[0]
    dens_vert = ratio * vert[1] - vert[0]
    floor = 16.0 * taper_eps / (thermal_coef * thermal_coef)
    slope = dens_side * dens_vert * reciprocal(dens_vert * dens_vert + floor)
    return [coeff * (grad[t] - slope * vert[t]) for t in range(2)]


def lane_roll(values, shift):
    return pltpu.roll(values, shift % Y, 1)


def row_roll(values, shift):
    return pltpu.roll(values, shift % values.shape[0], 0)


def south_depth(depth):
    lane = lax.broadcasted_iota(jnp.int32, depth.shape, 1)
    return jnp.where(lane == 0, 0, jnp.minimum(depth, lane_roll(depth, 1)))


def west_depth(depth):
    return jnp.minimum(depth, row_roll(depth, 1))


def pack_kernel(
    tracers, zonal, vertical, diffusivity, turbulence, sea, bottom,
    east_msg, west_msg, level_msg, depth_rows, sems
):
    slab = lax.axis_index("lev")
    first = (K - 2) * (1 - slab)
    copies = []

    def add(src, dst):
        copies.append(pltpu.make_async_copy(src, dst, sems.at[len(copies)]))
        copies[-1].start()

    for t in range(2):
        for i in range(2):
            rows = pl.ds((2 * t + i) * K, K)
            add(tracers.at[t, X - 2 + i], east_msg.at[rows])
            add(tracers.at[t, i], west_msg.at[rows])
            add(tracers.at[t, :, first + i, :], level_msg.at[2 * t + i])
    add(zonal.at[0], west_msg.at[pl.ds(4 * K, K)])
    add(diffusivity.at[0], west_msg.at[pl.ds(5 * K, K)])
    fifth = len(copies)
    upper = pltpu.make_async_copy(turbulence.at[:, K - 1, :], level_msg.at[4], sems.at[fifth])
    lower = pltpu.make_async_copy(vertical.at[:, 0, :], level_msg.at[4], sems.at[fifth])

    @pl.when(slab == 0)
    def _():
        upper.start()

    @pl.when(slab == 1)
    def _():
        lower.start()

    depth_rows[...] = (sea[...] * (bottom[...] + 1)).astype(F32)
    last = [
        pltpu.make_async_copy(depth_rows.at[pl.ds(8, 8)], east_msg.at[pl.ds(4 * K, 8)], sems.at[fifth + 1]),
        pltpu.make_async_copy(depth_rows.at[pl.ds(0, 8)], west_msg.at[pl.ds(6 * K, 8)], sems.at[fifth + 2]),
    ]
    for copy in last:
        copy.start()
    upper.wait()
    for copy in copies + last:
        copy.wait()


def interior_kernel(
    tracers, zonal, merid, vertical, diffusivity, turbulence, sea, bottom,
    p_first, p_second, inverse_out, carry_out, ratio_out, tail_out, cols, zcols, dcols, own_rows, extra_rows,
    fields, below_flux, grads_kept, sems, col_sems
):
    slab = lax.axis_index("lev")
    edge = (K - 1) * (1 - slab)
    base = K * slab

    def copies(k):
        turned = jnp.where(slab == 0, k, jnp.maximum(K - 2 - k, 0))
        pairs = [
            (tracers.at[:, :, k, :], fields.at[k, 0:2]),
            (zonal.at[:, k, :], fields.at[k, 2]),
            (merid.at[:, k, :], fields.at[k, 3]),
            (vertical.at[:, k, :], fields.at[k, 4]),
            (diffusivity.at[:, k, :], fields.at[k, 5]),
            (turbulence.at[:, turned, :], fields.at[k, 6]),
        ]
        return [pltpu.make_async_copy(a, b, sems.at[k]) for a, b in pairs]

    def arrive(k):
        pltpu.make_async_copy(fields.at[k], fields.at[k], sems.at[k]).wait()

    for k in range(AHEAD):
        for copy in copies(k):
            copy.start()

    depth = sea[...] * (bottom[...] + 1)
    depth_west = west_depth(depth)
    row = lax.broadcasted_iota(jnp.int32, (X, Y), 0)
    depth_west_inner = jnp.where((row >= 2) & (row <= X - 2), depth_west, 0)
    depth_south = south_depth(depth)
    column_copies = []

    def add(src, dst):
        column_copies.append(pltpu.make_async_copy(src, dst, col_sems.at[len(column_copies)]))
        column_copies[-1].start()

    for i, x in enumerate((0, 1, 2, X - 3, X - 2, X - 1)):
        for t in range(2):
            add(tracers.at[t, x], cols.at[t, i])
    for i, x in enumerate((0, 1, X - 1)):
        add(zonal.at[x], zcols.at[i])
        add(diffusivity.at[x], dcols.at[i])
    below_flux[...] = jnp.zeros_like(below_flux)
    tail_out[...] = jnp.zeros_like(tail_out)
    grads_kept[0] = jnp.zeros((2, X, Y), F32)

    for k in range(2):
        arrive(k)
    for t in range(2):
        grads_kept[1, t] = jnp.where(base + 1 < depth, fields[1, t] - fields[0, t], 0.0)

    def eliminate(j, tail, prev_rate):
        face = jnp.where(slab == 0, j + 1, 2 * K - 1 - j)
        turb = fields[j, 6]
        next_rate = jnp.where(face < depth, turb * lax.rsqrt(turb), 0.0)
        rest = 1.0 + prev_rate * tail
        inverse = reciprocal(rest + next_rate)
        inverse_out[j] = inverse
        carry_out[j] = prev_rate * inverse
        ratio_out[j] = next_rate * inverse
        return rest * inverse, next_rate

    def process(k, below, grad_up, grad_down):
        ahead = jnp.minimum(k + 2, K - 1)
        level = base + k
        down = jnp.minimum(k + 1, K - 1)
        here = [fields[k, t] for t in range(2)]
        next_row = [fields[down, t] for t in range(2)]
        open_far = jnp.where(k < K - 2, level + 2, FAR) < depth
        grad_far = [jnp.where(open_far, fields[ahead, t] - next_row[t], 0.0) for t in range(2)]
        centred = [grad_up[t] + grad_down[t] for t in range(2)]
        known = jnp.where(slab == 0, k < K - 2, k > 0)
        open_flux = jnp.where(known, level + 1, FAR) < depth
        down_courant = jnp.where(open_flux, fields[down, 4], 0.0)
        vert = face_flux(down_courant, here, grad_down, grad_up, grad_far)
        total = []
        for t in range(2):
            total.append(here[t] + below[t] - vert[t])
        iso_level = jnp.where(k == edge, FAR, level)
        spread = fields[k, 5]

        open_west = level < depth_west
        behind = [row_roll(here[t], 1) for t in range(2)]
        grad = [jnp.where(open_west, here[t] - behind[t], 0.0) for t in range(2)]
        flux = face_flux(
            jnp.where(level < depth_west_inner, fields[k, 2], 0.0),
            behind,
            grad,
            [row_roll(grad[t], 1) for t in range(2)],
            [row_roll(grad[t], -1) for t in range(2)],
        )
        iso = isoneutral(
            grad,
            [centred[t] + row_roll(centred[t], 1) for t in range(2)],
            jnp.where(iso_level < depth_west_inner, spread, 0.0),
        )
        for t in range(2):
            net = iso[t] - flux[t]
            total[t] = total[t] + (row_roll(net, -1) - net)

        open_south = level < depth_south
        behind = [lane_roll(here[t], 1) for t in range(2)]
        grad = [jnp.where(open_south, here[t] - behind[t], 0.0) for t in range(2)]
        flux = face_flux(
            jnp.where(open_south, fields[k, 3], 0.0),
            behind,
            grad,
            [lane_roll(grad[t], 1) for t in range(2)],
            [lane_roll(grad[t], -1) for t in range(2)],
        )
        iso = isoneutral(
            grad,
            [centred[t] + lane_roll(centred[t], 1) for t in range(2)],
            jnp.where(iso_level < depth_south, spread, 0.0),
        )
        for t in range(2):
            net = iso[t] - flux[t]
            total[t] = total[t] + (lane_roll(net, -1) - net)
            for lane in range(LANES):
                (p_first, p_second)[t][lane, pl.ds(k * X, X), :] = total[t][:, lane * 128 : lane * 128 + 128]
        return vert, grad_down, grad_far

    def step(i, start, wait):
        first = i * UNROLL
        for u in range(UNROLL):
            if start:
                for copy in copies(first + u + AHEAD):
                    copy.start()
            if wait:
                arrive(first + u + 2)
        below = [below_flux[t] for t in range(2)]
        grads = [[grads_kept[f, t] for t in range(2)] for f in range(2)]
        tail, prev_rate = tail_out[0], tail_out[1]
        for u in range(UNROLL):
            below, grad_down, grad_far = process(first + u, below, grads[0], grads[1])
            grads = [grad_down, grad_far]
            if wait or u < UNROLL - 1:
                tail, prev_rate = eliminate(first + u, tail, prev_rate)
        for t in range(2):
            below_flux[t] = below[t]
            for f in range(2):
                grads_kept[f, t] = grads[f][t]
        tail_out[0] = tail
        tail_out[1] = prev_rate

    steps = K // UNROLL
    fed = (K - AHEAD) // UNROLL

    @pl.loop(0, fed)
    def _(i):
        step(i, True, True)

    @pl.loop(fed, steps - 1)
    def _(i):
        step(i, False, True)

    step(steps - 1, False, False)
    for t in range(2):
        for i in range(3):
            own_rows[t, i] = fields[(K - 3) * (1 - slab) + i, t]
    extra_rows[0] = fields[edge, 4]
    extra_rows[1] = fields[1, 4]
    extra_rows[2] = fields[edge, 5]
    extra_rows[3] = fields[K - 1, 6]
    for copy in column_copies:
        copy.wait()


def edge_kernel(
    east_msg, west_msg, level_msg, sea, bottom,
    p_first, p_second, inverse, carry, tail, cols, zcols, dcols, own_rows, extra_rows,
    v_first, v_second, meet_out, corner_out,
    p, rows, sems
):
    slab = lax.axis_index("lev")
    edge = (K - 1) * (1 - slab)
    inner = 30 - 29 * slab
    base = K * slab
    fetches = [
        pltpu.make_async_copy(ref, p.at[t], sems.at[t]) for t, ref in enumerate((p_first, p_second))
    ]
    for fetch in fetches:
        fetch.start()
    for t in range(2):
        for i in range(3):
            rows[t, 2 * slab + i] = own_rows[t, i]
        for i in range(2):
            rows[t, 3 * (1 - slab) + i] = level_msg[2 * t + i]

    depth = sea[...] * (bottom[...] + 1)

    level = base + lax.broadcasted_iota(jnp.int32, (K, Y), 0)
    local_row = lax.broadcasted_iota(jnp.int32, (K, Y), 0)

    def zonal_edge(q, depths, halo, courants, spreads, outer_face):
        centred = []
        for i in range(3):
            column_depth = depths[i + 1]
            pair = []
            for t in range(2):
                mine = q[t][i + 1]
                outer = halo[t][i]
                below = jnp.where(local_row == K - 1, outer, row_roll(mine, -1))
                down = jnp.where(level + 1 < column_depth, below - mine, 0.0)
                top = jnp.where(
                    (slab == 1) & (level < column_depth), mine - outer, 0.0
                )
                up = jnp.where(local_row == 0, top, row_roll(down, 1))
                pair.append(up + down)
            centred.append(pair)
        opened = [level < jnp.minimum(depths[i], depths[i + 1]) for i in range(4)]
        grads = [
            [jnp.where(opened[i], q[t][i + 1] - q[t][i], 0.0) for t in range(2)] for i in range(4)
        ]
        nets = []
        for f in range(2):
            flux = face_flux(
                jnp.where(opened[f + 1], courants[f], 0.0),
                [q[t][f + 1] for t in range(2)],
                grads[f + 1],
                grads[f],
                grads[f + 2],
            )
            iso = isoneutral(
                grads[f + 1],
                [centred[f][t] + centred[f + 1][t] for t in range(2)],
                jnp.where(opened[f + 1] & (local_row != edge) if f == outer_face else opened[f + 1], spreads[f], 0.0),
            )
            nets.append([iso[t] - flux[t] for t in range(2)])
        return nets

    def add_column(t, x, values):
        for lane in range(LANES):
            where = (t, lane, pl.ds(x, K, stride=X), slice(None))
            p[where] = p[where] + values[:, lane * 128 : lane * 128 + 128]

    def depth_row(x):
        return depth[x : x + 1]

    def near(t, x):
        return level_msg[2 * t + slab, x : x + 1, :]

    west_depths = east_msg[4 * K : 4 * K + 8, :].astype(jnp.int32)
    nets = zonal_edge(
        [
            [east_msg[(2 * t + i) * K : (2 * t + i + 1) * K, :] for i in range(2)]
            + [cols[t, i] for i in range(3)]
            for t in range(2)
        ],
        [west_depths[6:7], west_depths[7:8], depth_row(0), depth_row(1), depth_row(2)],
        [[near(t, 0), near(t, 0), near(t, 1)] for t in range(2)],
        [zcols[0], zcols[1]],
        [dcols[0], dcols[1]],
        0,
    )
    for fetch in fetches:
        fetch.wait()
    for t in range(2):
        add_column(t, 0, nets[1][t] - nets[0][t])
        add_column(t, 1, -nets[1][t])
    east_depths = west_msg[6 * K : 6 * K + 8, :].astype(jnp.int32)
    nets = zonal_edge(
        [
            [cols[t, 3 + i] for i in range(3)]
            + [west_msg[(2 * t + i) * K : (2 * t + i + 1) * K, :] for i in range(2)]
            for t in range(2)
        ],
        [depth_row(X - 3), depth_row(X - 2), depth_row(X - 1), east_depths[0:1], east_depths[1:2]],
        [[near(t, X - 2), near(t, X - 1), near(t, X - 1)] for t in range(2)],
        [zcols[2], west_msg[4 * K : 5 * K, :]],
        [dcols[2], west_msg[5 * K : 6 * K, :]],
        1,
    )
    for t in range(2):
        add_column(t, X - 2, nets[0][t])
        add_column(t, X - 1, nets[1][t] - nets[0][t])

    start = K - 3 + slab
    q = [[rows[t, i] for i in range(5)] for t in range(2)]
    grads = [
        [jnp.where(start + i + 1 < depth, q[t][i + 1] - q[t][i], 0.0) for t in range(2)]
        for i in range(4)
    ]
    other = level_msg[4]
    courant_low = jnp.where(slab == 0, other, extra_rows[1])
    above = face_flux(
        jnp.where(start + 2 < depth, extra_rows[0], 0.0),
        [q[t][1] for t in range(2)], grads[1], grads[0], grads[2],
    )
    under = face_flux(
        jnp.where(start + 3 < depth, courant_low, 0.0),
        [q[t][2] for t in range(2)], grads[2], grads[1], grads[3],
    )
    centred = [grads[1][t] + grads[2][t] for t in range(2)]
    here = [q[t][2] for t in range(2)]
    mid = start + 2
    depth_west = west_depth(depth)
    row = lax.broadcasted_iota(jnp.int32, (X, Y), 0)
    depth_west_inner = jnp.where((row >= 2) & (row <= X - 2), depth_west, 0)
    depth_south = south_depth(depth)
    spread = extra_rows[2]
    grad = [jnp.where(mid < depth_west, here[t] - row_roll(here[t], 1), 0.0) for t in range(2)]
    zonal_iso = isoneutral(
        grad,
        [centred[t] + row_roll(centred[t], 1) for t in range(2)],
        jnp.where(mid < depth_west_inner, spread, 0.0),
    )
    grad = [jnp.where(mid < depth_south, here[t] - lane_roll(here[t], 1), 0.0) for t in range(2)]
    merid_iso = isoneutral(
        grad,
        [centred[t] + lane_roll(centred[t], 1) for t in range(2)],
        jnp.where(mid < depth_south, spread, 0.0),
    )

    def add_level(t, k, values):
        for lane in range(LANES):
            where = (t, lane, pl.ds(pl.multiple_of(k * X, X), X), slice(None))
            p[where] = p[where] + values[:, lane * 128 : lane * 128 + 128]

    for t in range(2):
        change = row_roll(zonal_iso[t], -1) - zonal_iso[t]
        change = change + (lane_roll(merid_iso[t], -1) - merid_iso[t])
        add_level(t, edge, change - (under[t] - above[t]))
        add_level(t, inner, jnp.where(slab == 0, -above[t], under[t]))

    def provisional(t, k):
        rows_at = pl.ds(pl.multiple_of(k * X, X), X)
        return jnp.concatenate([p[t, lane, rows_at, :] for lane in range(LANES)], axis=1)

    def forward(j, values):
        k = jnp.where(slab == 0, j, K - 1 - j)
        inv = inverse[j]
        car = carry[j]
        new = tuple(provisional(t, k) * inv + car * values[t] for t in range(2))
        for t in range(2):
            (v_first, v_second)[t][k] = new[t]
        return new

    zero = jnp.zeros((X, Y), F32)
    values = lax.fori_loop(0, K - 1, forward, (zero, zero))
    meet_rate = jnp.where(K < depth, jnp.sqrt(jnp.where(slab == 0, extra_rows[3], other)), 0.0)
    prev_rate = tail[1]
    rest = 1.0 + prev_rate * tail[0]
    inv = 1.0 / (rest + meet_rate)
    for t in range(2):
        meet_out[t] = (provisional(t, edge) + prev_rate * values[t]) * inv
    meet_out[2] = rest * inv

    corner_out[...] = jnp.zeros_like(corner_out)
    meet_out[3] = jnp.zeros((X, Y), F32)
    own_level = base + edge
    outside = ((east_msg, K, west_depths[7:8], 0), (west_msg, 0, east_depths[0:1], X - 1))
    open_inner = jnp.where(slab == 0, K - 1, K + 1)
    open_other = jnp.where(slab == 0, K + 1, K - 1)
    for side, (msg, offset, outer_depth, x) in enumerate(outside):
        column_depth = depth_row(x)
        for t in range(2):
            at_edge = offset + 2 * t * K + edge
            outer = msg[pl.ds(at_edge, 1), :]
            outer_inner = msg[pl.ds(offset + 2 * t * K + inner, 1), :]
            meet_out[3, 2 * t + side : 2 * t + side + 1, :] = outer
            meet_out[3, 4 + 2 * t + side : 5 + 2 * t + side, :] = jnp.where(
                open_inner < outer_depth, outer - outer_inner, 0.0
            )
            mine = own_rows[t, 2 * (1 - slab), x : x + 1, :]
            mine_inner = own_rows[t, 1, x : x + 1, :]
            theirs = near(t, x)
            theirs_inner = level_msg[2 * t + 1 - slab, x : x + 1, :]
            cross = jnp.where(K < column_depth, theirs - mine, 0.0)
            corner_out[t, side : side + 1, :] = mine
            corner_out[t, 2 + side : 3 + side, :] = theirs
            corner_out[2 + t, side : side + 1, :] = cross + jnp.where(
                open_inner < column_depth, mine - mine_inner, 0.0
            )
            corner_out[2 + t, 2 + side : 3 + side, :] = (
                jnp.where(open_other < column_depth, theirs - theirs_inner, 0.0) - cross
            )
        spread_row = dcols[0, pl.ds(edge, 1), :] if side == 0 else west_msg[pl.ds(5 * K + edge, 1), :]
        meet_out[3, 8 + side : 9 + side, :] = jnp.where(
            own_level < jnp.minimum(outer_depth, column_depth), spread_row, 0.0
        )
        meet_out[3, 10 + side : 11 + side, :] = inv[x : x + 1]
        shared = jnp.where(K < outer_depth, 1.0, 0.0)
        corner_out[4, side : side + 1, :] = shared
        corner_out[4, 2 + side : 3 + side, :] = shared


def finish_kernel(v_first, v_second, ratio, mine, theirs, corner, out, u, gathered, change, sems):
    slab = lax.axis_index("lev")
    for i in range(6):
        gathered[i, 0:2, :] = mine[3, 2 * i : 2 * i + 2, :]
        gathered[i, 2:4, :] = theirs[3, 2 * i : 2 * i + 2, :]
        gathered[i, 4:6, :] = theirs[3, 2 * i : 2 * i + 2, :]
        gathered[i, 6:8, :] = mine[3, 2 * i : 2 * i + 2, :]
    grad = []
    vert = []
    for t in range(2):
        outer = gathered[t]
        other = row_roll(outer, 4)
        grad.append(outer - corner[t])
        vert.append(corner[2 + t] + gathered[2 + t] + corner[4] * (other - outer))
    flux = isoneutral(grad, vert, gathered[4])
    change[...] = jnp.zeros_like(change)
    for t in range(2):
        moved = flux[t] * gathered[5]
        for i in range(2):
            change[i, t, 0:1, :] = moved[2 * i : 2 * i + 1]
            change[i, t, X - 1 : X, :] = moved[2 * i + 1 : 2 * i + 2]
    own_tail = mine[2]
    own_ratio = 1.0 - own_tail
    scale = reciprocal(own_tail + own_ratio * theirs[2])
    last = tuple(
        (mine[t] + change[0, t] + own_ratio * (theirs[t] + change[1, t])) * scale for t in range(2)
    )
    edge = (K - 1) * (1 - slab)

    def copies(k):
        return [pltpu.make_async_copy(u.at[:, k], out.at[:, :, k, :], sems.at[k])]

    for t in range(2):
        u[t, edge] = last[t]
    for copy in copies(edge):
        copy.start()

    def backward(i, values):
        j = K - 2 - i
        k = jnp.where(slab == 0, j, K - 1 - j)
        rat = ratio[j]
        new = tuple(v[k] + rat * values[t] for t, v in enumerate((v_first, v_second)))
        for t in range(2):
            u[t, k] = new[t]
        for copy in copies(k):
            copy.start()
        return new

    lax.fori_loop(0, K - 1, backward, last)

    @pl.loop(0, K)
    def _(k):
        for copy in copies(k):
            copy.wait()


def shape(*dims):
    return jax.ShapeDtypeStruct(dims, F32)


def params(mib):
    return pltpu.CompilerParams(vmem_limit_bytes=mib * 1024 * 1024)


def local(
    tracers, zonal, merid, vertical, diffusivity, turbulence, sea, bottom
):
    count = lax.axis_size("tile")
    east_msg, west_msg, level_msg = pl.pallas_call(
        pack_kernel,
        name="pack",
        in_specs=[any_spec()] * 5 + [vmem_spec()] * 2,
        out_specs=[vmem_spec()] * 3,
        out_shape=[shape(4 * K + 8, Y), shape(6 * K + 8, Y), shape(5, X, Y)],
        scratch_shapes=[pltpu.VMEM((X, Y), F32), pltpu.SemaphoreType.DMA((24,))],
        compiler_params=params(60),
    )(tracers, zonal, vertical, diffusivity, turbulence, sea, bottom)

    eastward = [(i, (i + 1) % count) for i in range(count)]
    east_in = lax.ppermute(east_msg, "tile", eastward)
    west_in = lax.ppermute(west_msg, "tile", [(b, a) for a, b in eastward])
    level_in = lax.ppermute(level_msg, "lev", [(0, 1), (1, 0)])

    p_first, p_second, inverse, carry, ratio, tail, *pieces = pl.pallas_call(
        interior_kernel,
        name="interior",
        in_specs=[any_spec()] * 6 + [vmem_spec()] * 2,
        out_specs=[vmem_spec()] * 11,
        out_shape=[
            shape(LANES, K * X, 128), shape(LANES, K * X, 128), shape(K, X, Y), shape(K, X, Y), shape(K, X, Y),
            shape(2, X, Y),
            shape(2, 6, K, Y), shape(3, K, Y), shape(3, K, Y), shape(2, 3, X, Y), shape(4, X, Y),
        ],
        scratch_shapes=[
            pltpu.VMEM((K, 7, X, Y), F32),
            pltpu.VMEM((2, X, Y), F32),
            pltpu.VMEM((2, 2, X, Y), F32),
            pltpu.SemaphoreType.DMA((K,)),
            pltpu.SemaphoreType.DMA((18,)),
        ],
        compiler_params=params(49),
        cost_estimate=pl.CostEstimate(flops=50_000_000, bytes_accessed=40_000_000, transcendentals=0),
    )(tracers, zonal, merid, vertical, diffusivity, turbulence, sea, bottom)

    v_first, v_second, meet, corner = pl.pallas_call(
        edge_kernel,
        name="edges",
        in_specs=[vmem_spec()] * 15,
        out_specs=[vmem_spec()] * 4,
        out_shape=[shape(K, X, Y), shape(K, X, Y), shape(4, X, Y), shape(5, 8, Y)],
        scratch_shapes=[
            pltpu.VMEM((2, LANES, K * X, 128), F32),
            pltpu.VMEM((2, 5, X, Y), F32),
            pltpu.SemaphoreType.DMA((2,)),
        ],
        compiler_params=params(46),
    )(east_in, west_in, level_in, sea, bottom, p_first, p_second, inverse, carry, tail, *pieces)

    meet_in = lax.ppermute(meet, "lev", [(0, 1), (1, 0)])
    return pl.pallas_call(
        finish_kernel,
        name="finish",
        in_specs=[vmem_spec()] * 6,
        out_specs=any_spec(),
        out_shape=shape(2, X, K, Y),
        scratch_shapes=[
            pltpu.VMEM((2, K, X, Y), F32),
            pltpu.VMEM((6, 8, Y), F32),
            pltpu.VMEM((2, 2, X, Y), F32),
            pltpu.SemaphoreType.DMA((K,)),
        ],
        compiler_params=params(46),
    )(v_first, v_second, ratio, meet, meet_in, corner)


def solution(mesh):
    return jax.shard_map(
        local,
        mesh=mesh,
        in_specs=(
            P(None, "tile", "lev", None),
            P("tile", "lev", None),
            P("tile", "lev", None),
            P("tile", "lev", None),
            P("tile", "lev", None),
            P("tile", "lev", None),
            P("tile", None),
            P("tile", None),
        ),
        out_specs=P(None, "tile", "lev", None),
        check_vma=False,
    )
```

```python
import jax
import jax.numpy as jnp
from jax import lax
from jax.experimental import pallas as pl
from jax.experimental.pallas import tpu as pltpu
from jax.sharding import PartitionSpec as P

thermal_coef = 0.2
haline_coef = 0.8
taper_eps = 0.05

X = 16
K = 32
Y = 384
LANES = 3
UNROLL = 2
AHEAD = 12
FAR = 1 << 20
F32 = jnp.float32


def any_spec():
    return pl.BlockSpec(memory_space=pl.ANY)


def vmem_spec():
    return pl.BlockSpec(memory_space=pltpu.VMEM)


def face_flux(courant, behind, grad, back, front):
    half = 0.5 * courant
    half_speed = jnp.abs(half)
    weight = half_speed - 2.0 * half_speed * half_speed
    lag = half - half_speed
    forward = courant > 0.0
    fluxes = []
    for t in range(2):
        upwind = jnp.where(forward, back[t], front[t])
        low = jnp.minimum(grad[t], 0.0)
        high = jnp.maximum(grad[t], 0.0)
        double = jnp.minimum(jnp.maximum(upwind + upwind, low), high)
        excess = jnp.minimum(jnp.maximum(upwind - grad[t], low), high)
        fluxes.append(courant * behind[t] + lag * grad[t] + weight * (double + excess))
    return fluxes


def reciprocal(values):
    guess = pl.reciprocal(values, approx=True)
    return guess * (2.0 - values * guess)


def isoneutral(grad, vert, coeff):
    ratio = haline_coef / thermal_coef
    dens_side = ratio * grad[1] - grad[0]
    dens_vert = ratio * vert[1] - vert[0]
    floor = 16.0 * taper_eps / (thermal_coef * thermal_coef)
    slope = dens_side * dens_vert * reciprocal(dens_vert * dens_vert + floor)
    return [coeff * (grad[t] - slope * vert[t]) for t in range(2)]


def lane_roll(values, shift):
    return pltpu.roll(values, shift % Y, 1)


def row_roll(values, shift):
    return pltpu.roll(values, shift % values.shape[0], 0)


def south_depth(depth):
    lane = lax.broadcasted_iota(jnp.int32, depth.shape, 1)
    return jnp.where(lane == 0, 0, jnp.minimum(depth, lane_roll(depth, 1)))


def west_depth(depth):
    return jnp.minimum(depth, row_roll(depth, 1))


def pack_kernel(
    tracers, zonal, vertical, diffusivity, turbulence, sea, bottom,
    east_msg, west_msg, level_msg, depth_rows, column, sems
):
    slab = lax.axis_index("lev")
    first = (K - 2) * (1 - slab)
    shapes = [
        pltpu.make_async_copy(ref, column.at[i], sems.at[20 + i]) for i, ref in enumerate((sea, bottom))
    ]
    for copy in shapes:
        copy.start()
    copies = []

    def add(src, dst):
        copies.append(pltpu.make_async_copy(src, dst, sems.at[len(copies)]))
        copies[-1].start()

    for t in range(2):
        for i in range(2):
            rows = pl.ds((2 * t + i) * K, K)
            add(tracers.at[t, X - 2 + i], east_msg.at[rows])
            add(tracers.at[t, i], west_msg.at[rows])
            add(tracers.at[t, :, first + i, :], level_msg.at[2 * t + i])
    add(zonal.at[0], west_msg.at[pl.ds(4 * K, K)])
    add(diffusivity.at[0], west_msg.at[pl.ds(5 * K, K)])
    fifth = len(copies)
    upper = pltpu.make_async_copy(turbulence.at[:, K - 1, :], level_msg.at[4], sems.at[fifth])
    lower = pltpu.make_async_copy(vertical.at[:, 0, :], level_msg.at[4], sems.at[fifth])

    @pl.when(slab == 0)
    def _():
        upper.start()

    @pl.when(slab == 1)
    def _():
        lower.start()

    for copy in shapes:
        copy.wait()
    depth_rows[...] = (column[0] * (column[1] + 1)).astype(F32)
    last = [
        pltpu.make_async_copy(depth_rows.at[pl.ds(8, 8)], east_msg.at[pl.ds(4 * K, 8)], sems.at[fifth + 1]),
        pltpu.make_async_copy(depth_rows.at[pl.ds(0, 8)], west_msg.at[pl.ds(6 * K, 8)], sems.at[fifth + 2]),
    ]
    for copy in last:
        copy.start()
    upper.wait()
    for copy in copies + last:
        copy.wait()


def interior_kernel(
    tracers, zonal, merid, vertical, diffusivity, turbulence, sea, bottom,
    p_first, p_second, inverse_out, carry_out, ratio_out, tail_out, cols, zcols, dcols, own_rows, extra_rows,
    fields, below_flux, grads_kept, column, sems, col_sems
):
    slab = lax.axis_index("lev")
    edge = (K - 1) * (1 - slab)
    base = K * slab

    def copies(k):
        turned = jnp.where(slab == 0, k, jnp.maximum(K - 2 - k, 0))
        pairs = [
            (tracers.at[:, :, k, :], fields.at[k, 0:2]),
            (zonal.at[:, k, :], fields.at[k, 2]),
            (merid.at[:, k, :], fields.at[k, 3]),
            (vertical.at[:, k, :], fields.at[k, 4]),
            (diffusivity.at[:, k, :], fields.at[k, 5]),
            (turbulence.at[:, turned, :], fields.at[k, 6]),
        ]
        return [pltpu.make_async_copy(a, b, sems.at[k]) for a, b in pairs]

    def arrive(k):
        pltpu.make_async_copy(fields.at[k], fields.at[k], sems.at[k]).wait()

    shapes = [
        pltpu.make_async_copy(ref, column.at[i], col_sems.at[18 + i]) for i, ref in enumerate((sea, bottom))
    ]
    for copy in shapes:
        copy.start()
    for k in range(AHEAD):
        for copy in copies(k):
            copy.start()
    for copy in shapes:
        copy.wait()

    depth = column[0] * (column[1] + 1)
    depth_west = west_depth(depth)
    row = lax.broadcasted_iota(jnp.int32, (X, Y), 0)
    depth_west_inner = jnp.where((row >= 2) & (row <= X - 2), depth_west, 0)
    depth_south = south_depth(depth)
    column_copies = []

    def add(src, dst):
        column_copies.append(pltpu.make_async_copy(src, dst, col_sems.at[len(column_copies)]))
        column_copies[-1].start()

    for i, x in enumerate((0, 1, 2, X - 3, X - 2, X - 1)):
        for t in range(2):
            add(tracers.at[t, x], cols.at[t, i])
    for i, x in enumerate((0, 1, X - 1)):
        add(zonal.at[x], zcols.at[i])
        add(diffusivity.at[x], dcols.at[i])
    below_flux[...] = jnp.zeros_like(below_flux)
    tail_out[...] = jnp.zeros_like(tail_out)
    grads_kept[0] = jnp.zeros((2, X, Y), F32)

    for k in range(2):
        arrive(k)
    for t in range(2):
        grads_kept[1, t] = jnp.where(base + 1 < depth, fields[1, t] - fields[0, t], 0.0)

    def eliminate(j, tail, prev_rate):
        face = jnp.where(slab == 0, j + 1, 2 * K - 1 - j)
        turb = fields[j, 6]
        next_rate = jnp.where(face < depth, turb * lax.rsqrt(turb), 0.0)
        rest = 1.0 + prev_rate * tail
        inverse = reciprocal(rest + next_rate)
        inverse_out[j] = inverse
        carry_out[j] = prev_rate * inverse
        ratio_out[j] = next_rate * inverse
        return rest * inverse, next_rate

    def process(k, below, grad_up, grad_down):
        ahead = jnp.minimum(k + 2, K - 1)
        level = base + k
        down = jnp.minimum(k + 1, K - 1)
        here = [fields[k, t] for t in range(2)]
        next_row = [fields[down, t] for t in range(2)]
        open_far = jnp.where(k < K - 2, level + 2, FAR) < depth
        grad_far = [jnp.where(open_far, fields[ahead, t] - next_row[t], 0.0) for t in range(2)]
        centred = [grad_up[t] + grad_down[t] for t in range(2)]
        known = jnp.where(slab == 0, k < K - 2, k > 0)
        open_flux = jnp.where(known, level + 1, FAR) < depth
        down_courant = jnp.where(open_flux, fields[down, 4], 0.0)
        vert = face_flux(down_courant, here, grad_down, grad_up, grad_far)
        total = []
        for t in range(2):
            total.append(here[t] + below[t] - vert[t])
        iso_level = jnp.where(k == edge, FAR, level)
        spread = fields[k, 5]

        open_west = level < depth_west
        behind = [row_roll(here[t], 1) for t in range(2)]
        grad = [jnp.where(open_west, here[t] - behind[t], 0.0) for t in range(2)]
        flux = face_flux(
            jnp.where(level < depth_west_inner, fields[k, 2], 0.0),
            behind,
            grad,
            [row_roll(grad[t], 1) for t in range(2)],
            [row_roll(grad[t], -1) for t in range(2)],
        )
        iso = isoneutral(
            grad,
            [centred[t] + row_roll(centred[t], 1) for t in range(2)],
            jnp.where(iso_level < depth_west_inner, spread, 0.0),
        )
        for t in range(2):
            net = iso[t] - flux[t]
            total[t] = total[t] + (row_roll(net, -1) - net)

        open_south = level < depth_south
        behind = [lane_roll(here[t], 1) for t in range(2)]
        grad = [jnp.where(open_south, here[t] - behind[t], 0.0) for t in range(2)]
        flux = face_flux(
            jnp.where(open_south, fields[k, 3], 0.0),
            behind,
            grad,
            [lane_roll(grad[t], 1) for t in range(2)],
            [lane_roll(grad[t], -1) for t in range(2)],
        )
        iso = isoneutral(
            grad,
            [centred[t] + lane_roll(centred[t], 1) for t in range(2)],
            jnp.where(iso_level < depth_south, spread, 0.0),
        )
        for t in range(2):
            net = iso[t] - flux[t]
            total[t] = total[t] + (lane_roll(net, -1) - net)
            for lane in range(LANES):
                (p_first, p_second)[t][lane, pl.ds(k * X, X), :] = total[t][:, lane * 128 : lane * 128 + 128]
        return vert, grad_down, grad_far

    def step(i, start, wait):
        first = i * UNROLL
        for u in range(UNROLL):
            if start:
                for copy in copies(first + u + AHEAD):
                    copy.start()
            if wait:
                arrive(first + u + 2)
        below = [below_flux[t] for t in range(2)]
        grads = [[grads_kept[f, t] for t in range(2)] for f in range(2)]
        tail, prev_rate = tail_out[0], tail_out[1]
        for u in range(UNROLL):
            below, grad_down, grad_far = process(first + u, below, grads[0], grads[1])
            grads = [grad_down, grad_far]
            if wait or u < UNROLL - 1:
                tail, prev_rate = eliminate(first + u, tail, prev_rate)
        for t in range(2):
            below_flux[t] = below[t]
            for f in range(2):
                grads_kept[f, t] = grads[f][t]
        tail_out[0] = tail
        tail_out[1] = prev_rate

    steps = K // UNROLL
    fed = (K - AHEAD) // UNROLL

    @pl.loop(0, fed)
    def _(i):
        step(i, True, True)

    @pl.loop(fed, steps - 1)
    def _(i):
        step(i, False, True)

    step(steps - 1, False, False)
    for t in range(2):
        for i in range(3):
            own_rows[t, i] = fields[(K - 3) * (1 - slab) + i, t]
    extra_rows[0] = fields[edge, 4]
    extra_rows[1] = fields[1, 4]
    extra_rows[2] = fields[edge, 5]
    extra_rows[3] = fields[K - 1, 6]
    for copy in column_copies:
        copy.wait()


def edge_kernel(
    east_msg, west_msg, level_msg, sea, bottom,
    p_first, p_second, inverse, carry, tail, cols, zcols, dcols, own_rows, extra_rows,
    v_first, v_second, meet_out, corner_out,
    p, rows, sems
):
    slab = lax.axis_index("lev")
    edge = (K - 1) * (1 - slab)
    inner = 30 - 29 * slab
    base = K * slab
    fetches = [
        pltpu.make_async_copy(ref, p.at[t], sems.at[t]) for t, ref in enumerate((p_first, p_second))
    ]
    for fetch in fetches:
        fetch.start()
    for t in range(2):
        for i in range(3):
            rows[t, 2 * slab + i] = own_rows[t, i]
        for i in range(2):
            rows[t, 3 * (1 - slab) + i] = level_msg[2 * t + i]

    depth = sea[...] * (bottom[...] + 1)

    level = base + lax.broadcasted_iota(jnp.int32, (K, Y), 0)
    local_row = lax.broadcasted_iota(jnp.int32, (K, Y), 0)

    def zonal_edge(q, depths, halo, courants, spreads, outer_face):
        centred = []
        for i in range(3):
            column_depth = depths[i + 1]
            pair = []
            for t in range(2):
                mine = q[t][i + 1]
                outer = halo[t][i]
                below = jnp.where(local_row == K - 1, outer, row_roll(mine, -1))
                down = jnp.where(level + 1 < column_depth, below - mine, 0.0)
                top = jnp.where(
                    (slab == 1) & (level < column_depth), mine - outer, 0.0
                )
                up = jnp.where(local_row == 0, top, row_roll(down, 1))
                pair.append(up + down)
            centred.append(pair)
        opened = [level < jnp.minimum(depths[i], depths[i + 1]) for i in range(4)]
        grads = [
            [jnp.where(opened[i], q[t][i + 1] - q[t][i], 0.0) for t in range(2)] for i in range(4)
        ]
        nets = []
        for f in range(2):
            flux = face_flux(
                jnp.where(opened[f + 1], courants[f], 0.0),
                [q[t][f + 1] for t in range(2)],
                grads[f + 1],
                grads[f],
                grads[f + 2],
            )
            iso = isoneutral(
                grads[f + 1],
                [centred[f][t] + centred[f + 1][t] for t in range(2)],
                jnp.where(opened[f + 1] & (local_row != edge) if f == outer_face else opened[f + 1], spreads[f], 0.0),
            )
            nets.append([iso[t] - flux[t] for t in range(2)])
        return nets

    def add_column(t, x, values):
        for lane in range(LANES):
            where = (t, lane, pl.ds(x, K, stride=X), slice(None))
            p[where] = p[where] + values[:, lane * 128 : lane * 128 + 128]

    def depth_row(x):
        return depth[x : x + 1]

    def near(t, x):
        return level_msg[2 * t + slab, x : x + 1, :]

    west_depths = east_msg[4 * K : 4 * K + 8, :].astype(jnp.int32)
    nets = zonal_edge(
        [
            [east_msg[(2 * t + i) * K : (2 * t + i + 1) * K, :] for i in range(2)]
            + [cols[t, i] for i in range(3)]
            for t in range(2)
        ],
        [west_depths[6:7], west_depths[7:8], depth_row(0), depth_row(1), depth_row(2)],
        [[near(t, 0), near(t, 0), near(t, 1)] for t in range(2)],
        [zcols[0], zcols[1]],
        [dcols[0], dcols[1]],
        0,
    )
    for fetch in fetches:
        fetch.wait()
    for t in range(2):
        add_column(t, 0, nets[1][t] - nets[0][t])
        add_column(t, 1, -nets[1][t])
    east_depths = west_msg[6 * K : 6 * K + 8, :].astype(jnp.int32)
    nets = zonal_edge(
        [
            [cols[t, 3 + i] for i in range(3)]
            + [west_msg[(2 * t + i) * K : (2 * t + i + 1) * K, :] for i in range(2)]
            for t in range(2)
        ],
        [depth_row(X - 3), depth_row(X - 2), depth_row(X - 1), east_depths[0:1], east_depths[1:2]],
        [[near(t, X - 2), near(t, X - 1), near(t, X - 1)] for t in range(2)],
        [zcols[2], west_msg[4 * K : 5 * K, :]],
        [dcols[2], west_msg[5 * K : 6 * K, :]],
        1,
    )
    for t in range(2):
        add_column(t, X - 2, nets[0][t])
        add_column(t, X - 1, nets[1][t] - nets[0][t])

    start = K - 3 + slab
    q = [[rows[t, i] for i in range(5)] for t in range(2)]
    grads = [
        [jnp.where(start + i + 1 < depth, q[t][i + 1] - q[t][i], 0.0) for t in range(2)]
        for i in range(4)
    ]
    other = level_msg[4]
    courant_low = jnp.where(slab == 0, other, extra_rows[1])
    above = face_flux(
        jnp.where(start + 2 < depth, extra_rows[0], 0.0),
        [q[t][1] for t in range(2)], grads[1], grads[0], grads[2],
    )
    under = face_flux(
        jnp.where(start + 3 < depth, courant_low, 0.0),
        [q[t][2] for t in range(2)], grads[2], grads[1], grads[3],
    )
    centred = [grads[1][t] + grads[2][t] for t in range(2)]
    here = [q[t][2] for t in range(2)]
    mid = start + 2
    depth_west = west_depth(depth)
    row = lax.broadcasted_iota(jnp.int32, (X, Y), 0)
    depth_west_inner = jnp.where((row >= 2) & (row <= X - 2), depth_west, 0)
    depth_south = south_depth(depth)
    spread = extra_rows[2]
    grad = [jnp.where(mid < depth_west, here[t] - row_roll(here[t], 1), 0.0) for t in range(2)]
    zonal_iso = isoneutral(
        grad,
        [centred[t] + row_roll(centred[t], 1) for t in range(2)],
        jnp.where(mid < depth_west_inner, spread, 0.0),
    )
    grad = [jnp.where(mid < depth_south, here[t] - lane_roll(here[t], 1), 0.0) for t in range(2)]
    merid_iso = isoneutral(
        grad,
        [centred[t] + lane_roll(centred[t], 1) for t in range(2)],
        jnp.where(mid < depth_south, spread, 0.0),
    )

    def add_level(t, k, values):
        for lane in range(LANES):
            where = (t, lane, pl.ds(pl.multiple_of(k * X, X), X), slice(None))
            p[where] = p[where] + values[:, lane * 128 : lane * 128 + 128]

    for t in range(2):
        change = row_roll(zonal_iso[t], -1) - zonal_iso[t]
        change = change + (lane_roll(merid_iso[t], -1) - merid_iso[t])
        add_level(t, edge, change - (under[t] - above[t]))
        add_level(t, inner, jnp.where(slab == 0, -above[t], under[t]))

    def provisional(t, k):
        rows_at = pl.ds(pl.multiple_of(k * X, X), X)
        return jnp.concatenate([p[t, lane, rows_at, :] for lane in range(LANES)], axis=1)

    def forward(j, values):
        k = jnp.where(slab == 0, j, K - 1 - j)
        inv = inverse[j]
        car = carry[j]
        new = tuple(provisional(t, k) * inv + car * values[t] for t in range(2))
        for t in range(2):
            (v_first, v_second)[t][k] = new[t]
        return new

    zero = jnp.zeros((X, Y), F32)
    values = lax.fori_loop(0, K - 1, forward, (zero, zero))
    meet_rate = jnp.where(K < depth, jnp.sqrt(jnp.where(slab == 0, extra_rows[3], other)), 0.0)
    prev_rate = tail[1]
    rest = 1.0 + prev_rate * tail[0]
    inv = 1.0 / (rest + meet_rate)
    for t in range(2):
        meet_out[t] = (provisional(t, edge) + prev_rate * values[t]) * inv
    meet_out[2] = rest * inv

    corner_out[...] = jnp.zeros_like(corner_out)
    meet_out[3] = jnp.zeros((X, Y), F32)
    own_level = base + edge
    outside = ((east_msg, K, west_depths[7:8], 0), (west_msg, 0, east_depths[0:1], X - 1))
    open_inner = jnp.where(slab == 0, K - 1, K + 1)
    open_other = jnp.where(slab == 0, K + 1, K - 1)
    for side, (msg, offset, outer_depth, x) in enumerate(outside):
        column_depth = depth_row(x)
        for t in range(2):
            at_edge = offset + 2 * t * K + edge
            outer = msg[pl.ds(at_edge, 1), :]
            outer_inner = msg[pl.ds(offset + 2 * t * K + inner, 1), :]
            meet_out[3, 2 * t + side : 2 * t + side + 1, :] = outer
            meet_out[3, 4 + 2 * t + side : 5 + 2 * t + side, :] = jnp.where(
                open_inner < outer_depth, outer - outer_inner, 0.0
            )
            mine = own_rows[t, 2 * (1 - slab), x : x + 1, :]
            mine_inner = own_rows[t, 1, x : x + 1, :]
            theirs = near(t, x)
            theirs_inner = level_msg[2 * t + 1 - slab, x : x + 1, :]
            cross = jnp.where(K < column_depth, theirs - mine, 0.0)
            corner_out[t, side : side + 1, :] = mine
            corner_out[t, 2 + side : 3 + side, :] = theirs
            corner_out[2 + t, side : side + 1, :] = cross + jnp.where(
                open_inner < column_depth, mine - mine_inner, 0.0
            )
            corner_out[2 + t, 2 + side : 3 + side, :] = (
                jnp.where(open_other < column_depth, theirs - theirs_inner, 0.0) - cross
            )
        spread_row = dcols[0, pl.ds(edge, 1), :] if side == 0 else west_msg[pl.ds(5 * K + edge, 1), :]
        meet_out[3, 8 + side : 9 + side, :] = jnp.where(
            own_level < jnp.minimum(outer_depth, column_depth), spread_row, 0.0
        )
        meet_out[3, 10 + side : 11 + side, :] = inv[x : x + 1]
        shared = jnp.where(K < outer_depth, 1.0, 0.0)
        corner_out[4, side : side + 1, :] = shared
        corner_out[4, 2 + side : 3 + side, :] = shared


def finish_kernel(v_first, v_second, ratio, mine, theirs, corner, out, u, gathered, change, sems):
    slab = lax.axis_index("lev")
    for i in range(6):
        gathered[i, 0:2, :] = mine[3, 2 * i : 2 * i + 2, :]
        gathered[i, 2:4, :] = theirs[3, 2 * i : 2 * i + 2, :]
        gathered[i, 4:6, :] = theirs[3, 2 * i : 2 * i + 2, :]
        gathered[i, 6:8, :] = mine[3, 2 * i : 2 * i + 2, :]
    grad = []
    vert = []
    for t in range(2):
        outer = gathered[t]
        other = row_roll(outer, 4)
        grad.append(outer - corner[t])
        vert.append(corner[2 + t] + gathered[2 + t] + corner[4] * (other - outer))
    flux = isoneutral(grad, vert, gathered[4])
    change[...] = jnp.zeros_like(change)
    for t in range(2):
        moved = flux[t] * gathered[5]
        for i in range(2):
            change[i, t, 0:1, :] = moved[2 * i : 2 * i + 1]
            change[i, t, X - 1 : X, :] = moved[2 * i + 1 : 2 * i + 2]
    own_tail = mine[2]
    own_ratio = 1.0 - own_tail
    scale = reciprocal(own_tail + own_ratio * theirs[2])
    last = tuple(
        (mine[t] + change[0, t] + own_ratio * (theirs[t] + change[1, t])) * scale for t in range(2)
    )
    edge = (K - 1) * (1 - slab)

    def copies(k):
        return [pltpu.make_async_copy(u.at[:, k], out.at[:, :, k, :], sems.at[k])]

    for t in range(2):
        u[t, edge] = last[t]
    for copy in copies(edge):
        copy.start()

    def backward(i, values):
        j = K - 2 - i
        k = jnp.where(slab == 0, j, K - 1 - j)
        rat = ratio[j]
        new = tuple(v[k] + rat * values[t] for t, v in enumerate((v_first, v_second)))
        for t in range(2):
            u[t, k] = new[t]
        for copy in copies(k):
            copy.start()
        return new

    lax.fori_loop(0, K - 1, backward, last)

    @pl.loop(0, K)
    def _(k):
        for copy in copies(k):
            copy.wait()


def shape(*dims):
    return jax.ShapeDtypeStruct(dims, F32)


def params(mib):
    return pltpu.CompilerParams(vmem_limit_bytes=mib * 1024 * 1024)


def local(
    tracers, zonal, merid, vertical, diffusivity, turbulence, sea, bottom
):
    count = lax.axis_size("tile")
    east_msg, west_msg, level_msg = pl.pallas_call(
        pack_kernel,
        name="pack",
        in_specs=[any_spec()] * 7,
        out_specs=[vmem_spec()] * 3,
        out_shape=[shape(4 * K + 8, Y), shape(6 * K + 8, Y), shape(5, X, Y)],
        scratch_shapes=[
            pltpu.VMEM((X, Y), F32), pltpu.VMEM((2, X, Y), jnp.int32), pltpu.SemaphoreType.DMA((24,))
        ],
        compiler_params=params(60),
    )(tracers, zonal, vertical, diffusivity, turbulence, sea, bottom)

    eastward = [(i, (i + 1) % count) for i in range(count)]
    east_in = lax.ppermute(east_msg, "tile", eastward)
    west_in = lax.ppermute(west_msg, "tile", [(b, a) for a, b in eastward])
    level_in = lax.ppermute(level_msg, "lev", [(0, 1), (1, 0)])

    p_first, p_second, inverse, carry, ratio, tail, *pieces = pl.pallas_call(
        interior_kernel,
        name="interior",
        in_specs=[any_spec()] * 8,
        out_specs=[vmem_spec()] * 11,
        out_shape=[
            shape(LANES, K * X, 128), shape(LANES, K * X, 128), shape(K, X, Y), shape(K, X, Y), shape(K, X, Y),
            shape(2, X, Y),
            shape(2, 6, K, Y), shape(3, K, Y), shape(3, K, Y), shape(2, 3, X, Y), shape(4, X, Y),
        ],
        scratch_shapes=[
            pltpu.VMEM((K, 7, X, Y), F32),
            pltpu.VMEM((2, X, Y), F32),
            pltpu.VMEM((2, 2, X, Y), F32),
            pltpu.VMEM((2, X, Y), jnp.int32),
            pltpu.SemaphoreType.DMA((K,)),
            pltpu.SemaphoreType.DMA((20,)),
        ],
        compiler_params=params(49),
        cost_estimate=pl.CostEstimate(flops=50_000_000, bytes_accessed=40_000_000, transcendentals=0),
    )(tracers, zonal, merid, vertical, diffusivity, turbulence, sea, bottom)

    v_first, v_second, meet, corner = pl.pallas_call(
        edge_kernel,
        name="edges",
        in_specs=[vmem_spec()] * 15,
        out_specs=[vmem_spec()] * 4,
        out_shape=[shape(K, X, Y), shape(K, X, Y), shape(4, X, Y), shape(5, 8, Y)],
        scratch_shapes=[
            pltpu.VMEM((2, LANES, K * X, 128), F32),
            pltpu.VMEM((2, 5, X, Y), F32),
            pltpu.SemaphoreType.DMA((2,)),
        ],
        compiler_params=params(46),
    )(east_in, west_in, level_in, sea, bottom, p_first, p_second, inverse, carry, tail, *pieces)

    meet_in = lax.ppermute(meet, "lev", [(0, 1), (1, 0)])
    return pl.pallas_call(
        finish_kernel,
        name="finish",
        in_specs=[vmem_spec()] * 6,
        out_specs=any_spec(),
        out_shape=shape(2, X, K, Y),
        scratch_shapes=[
            pltpu.VMEM((2, K, X, Y), F32),
            pltpu.VMEM((6, 8, Y), F32),
            pltpu.VMEM((2, 2, X, Y), F32),
            pltpu.SemaphoreType.DMA((K,)),
        ],
        compiler_params=params(46),
    )(v_first, v_second, ratio, meet, meet_in, corner)


def solution(mesh):
    return jax.shard_map(
        local,
        mesh=mesh,
        in_specs=(
            P(None, "tile", "lev", None),
            P("tile", "lev", None),
            P("tile", "lev", None),
            P("tile", "lev", None),
            P("tile", "lev", None),
            P("tile", "lev", None),
            P("tile", None),
            P("tile", None),
        ),
        out_specs=P(None, "tile", "lev", None),
        check_vma=False,
    )
```

```python
import jax
import jax.numpy as jnp
from jax import lax
from jax.experimental import pallas as pl
from jax.experimental.pallas import tpu as pltpu
from jax.sharding import PartitionSpec as P

thermal_coef = 0.2
haline_coef = 0.8
taper_eps = 0.05

X = 16
K = 32
Y = 384
LANES = 3
UNROLL = 2
AHEAD = 24
FAR = 1 << 20
F32 = jnp.float32


def any_spec():
    return pl.BlockSpec(memory_space=pl.ANY)


def vmem_spec():
    return pl.BlockSpec(memory_space=pltpu.VMEM)


def face_flux(courant, behind, grad, back, front):
    half = 0.5 * courant
    half_speed = jnp.abs(half)
    weight = half_speed - 2.0 * half_speed * half_speed
    lag = half - half_speed
    forward = courant > 0.0
    fluxes = []
    for t in range(2):
        upwind = jnp.where(forward, back[t], front[t])
        low = jnp.minimum(grad[t], 0.0)
        high = jnp.maximum(grad[t], 0.0)
        double = jnp.minimum(jnp.maximum(upwind + upwind, low), high)
        excess = jnp.minimum(jnp.maximum(upwind - grad[t], low), high)
        fluxes.append(courant * behind[t] + lag * grad[t] + weight * (double + excess))
    return fluxes


def reciprocal(values):
    guess = pl.reciprocal(values, approx=True)
    return guess * (2.0 - values * guess)


def isoneutral(grad, vert, coeff):
    ratio = haline_coef / thermal_coef
    dens_side = ratio * grad[1] - grad[0]
    dens_vert = ratio * vert[1] - vert[0]
    floor = 16.0 * taper_eps / (thermal_coef * thermal_coef)
    slope = dens_side * dens_vert * reciprocal(dens_vert * dens_vert + floor)
    return [coeff * (grad[t] - slope * vert[t]) for t in range(2)]


def lane_roll(values, shift):
    return pltpu.roll(values, shift % Y, 1)


def row_roll(values, shift):
    return pltpu.roll(values, shift % values.shape[0], 0)


def south_depth(depth):
    lane = lax.broadcasted_iota(jnp.int32, depth.shape, 1)
    return jnp.where(lane == 0, 0, jnp.minimum(depth, lane_roll(depth, 1)))


def west_depth(depth):
    return jnp.minimum(depth, row_roll(depth, 1))


def pack_kernel(
    tracers, zonal, vertical, diffusivity, turbulence, sea, bottom,
    east_msg, west_msg, level_msg, depth_rows, column, sems
):
    slab = lax.axis_index("lev")
    first = (K - 2) * (1 - slab)
    shapes = [
        pltpu.make_async_copy(ref, column.at[i], sems.at[20 + i]) for i, ref in enumerate((sea, bottom))
    ]
    for copy in shapes:
        copy.start()
    copies = []

    def add(src, dst):
        copies.append(pltpu.make_async_copy(src, dst, sems.at[len(copies)]))
        copies[-1].start()

    for t in range(2):
        for i in range(2):
            rows = pl.ds((2 * t + i) * K, K)
            add(tracers.at[t, X - 2 + i], east_msg.at[rows])
            add(tracers.at[t, i], west_msg.at[rows])
            add(tracers.at[t, :, first + i, :], level_msg.at[2 * t + i])
    add(zonal.at[0], west_msg.at[pl.ds(4 * K, K)])
    add(diffusivity.at[0], west_msg.at[pl.ds(5 * K, K)])
    fifth = len(copies)
    upper = pltpu.make_async_copy(turbulence.at[:, K - 1, :], level_msg.at[4], sems.at[fifth])
    lower = pltpu.make_async_copy(vertical.at[:, 0, :], level_msg.at[4], sems.at[fifth])

    @pl.when(slab == 0)
    def _():
        upper.start()

    @pl.when(slab == 1)
    def _():
        lower.start()

    for copy in shapes:
        copy.wait()
    depth_rows[...] = (column[0] * (column[1] + 1)).astype(F32)
    last = [
        pltpu.make_async_copy(depth_rows.at[pl.ds(8, 8)], east_msg.at[pl.ds(4 * K, 8)], sems.at[fifth + 1]),
        pltpu.make_async_copy(depth_rows.at[pl.ds(0, 8)], west_msg.at[pl.ds(6 * K, 8)], sems.at[fifth + 2]),
    ]
    for copy in last:
        copy.start()
    upper.wait()
    for copy in copies + last:
        copy.wait()


def interior_kernel(
    tracers, zonal, merid, vertical, diffusivity, turbulence, sea, bottom,
    p_first, p_second, inverse_out, carry_out, ratio_out, tail_out, cols, zcols, dcols, own_rows, extra_rows,
    fields, below_flux, grads_kept, column, sems, col_sems
):
    slab = lax.axis_index("lev")
    edge = (K - 1) * (1 - slab)
    base = K * slab

    def copies(k):
        turned = jnp.where(slab == 0, k, jnp.maximum(K - 2 - k, 0))
        pairs = [
            (tracers.at[:, :, k, :], fields.at[k, 0:2]),
            (zonal.at[:, k, :], fields.at[k, 2]),
            (merid.at[:, k, :], fields.at[k, 3]),
            (vertical.at[:, k, :], fields.at[k, 4]),
            (diffusivity.at[:, k, :], fields.at[k, 5]),
            (turbulence.at[:, turned, :], fields.at[k, 6]),
        ]
        return [pltpu.make_async_copy(a, b, sems.at[k]) for a, b in pairs]

    def arrive(k):
        pltpu.make_async_copy(fields.at[k], fields.at[k], sems.at[k]).wait()

    shapes = [
        pltpu.make_async_copy(ref, column.at[i], col_sems.at[18 + i]) for i, ref in enumerate((sea, bottom))
    ]
    for copy in shapes:
        copy.start()
    for k in range(AHEAD):
        for copy in copies(k):
            copy.start()
    for copy in shapes:
        copy.wait()

    depth = column[0] * (column[1] + 1)
    depth_west = west_depth(depth)
    row = lax.broadcasted_iota(jnp.int32, (X, Y), 0)
    depth_west_inner = jnp.where((row >= 2) & (row <= X - 2), depth_west, 0)
    depth_south = south_depth(depth)
    column_copies = []

    def add(src, dst):
        column_copies.append(pltpu.make_async_copy(src, dst, col_sems.at[len(column_copies)]))
        column_copies[-1].start()

    for i, x in enumerate((0, 1, 2, X - 3, X - 2, X - 1)):
        for t in range(2):
            add(tracers.at[t, x], cols.at[t, i])
    for i, x in enumerate((0, 1, X - 1)):
        add(zonal.at[x], zcols.at[i])
        add(diffusivity.at[x], dcols.at[i])
    below_flux[...] = jnp.zeros_like(below_flux)
    tail_out[...] = jnp.zeros_like(tail_out)
    grads_kept[0] = jnp.zeros((2, X, Y), F32)

    for k in range(2):
        arrive(k)
    for t in range(2):
        grads_kept[1, t] = jnp.where(base + 1 < depth, fields[1, t] - fields[0, t], 0.0)

    def eliminate(j, tail, prev_rate):
        face = jnp.where(slab == 0, j + 1, 2 * K - 1 - j)
        turb = fields[j, 6]
        next_rate = jnp.where(face < depth, turb * lax.rsqrt(turb), 0.0)
        rest = 1.0 + prev_rate * tail
        inverse = reciprocal(rest + next_rate)
        inverse_out[j] = inverse
        carry_out[j] = prev_rate * inverse
        ratio_out[j] = next_rate * inverse
        return rest * inverse, next_rate

    def process(k, below, grad_up, grad_down):
        ahead = jnp.minimum(k + 2, K - 1)
        level = base + k
        down = jnp.minimum(k + 1, K - 1)
        here = [fields[k, t] for t in range(2)]
        next_row = [fields[down, t] for t in range(2)]
        open_far = jnp.where(k < K - 2, level + 2, FAR) < depth
        grad_far = [jnp.where(open_far, fields[ahead, t] - next_row[t], 0.0) for t in range(2)]
        centred = [grad_up[t] + grad_down[t] for t in range(2)]
        known = jnp.where(slab == 0, k < K - 2, k > 0)
        open_flux = jnp.where(known, level + 1, FAR) < depth
        down_courant = jnp.where(open_flux, fields[down, 4], 0.0)
        vert = face_flux(down_courant, here, grad_down, grad_up, grad_far)
        total = []
        for t in range(2):
            total.append(here[t] + below[t] - vert[t])
        iso_level = jnp.where(k == edge, FAR, level)
        spread = fields[k, 5]

        open_west = level < depth_west
        behind = [row_roll(here[t], 1) for t in range(2)]
        grad = [jnp.where(open_west, here[t] - behind[t], 0.0) for t in range(2)]
        flux = face_flux(
            jnp.where(level < depth_west_inner, fields[k, 2], 0.0),
            behind,
            grad,
            [row_roll(grad[t], 1) for t in range(2)],
            [row_roll(grad[t], -1) for t in range(2)],
        )
        iso = isoneutral(
            grad,
            [centred[t] + row_roll(centred[t], 1) for t in range(2)],
            jnp.where(iso_level < depth_west_inner, spread, 0.0),
        )
        for t in range(2):
            net = iso[t] - flux[t]
            total[t] = total[t] + (row_roll(net, -1) - net)

        open_south = level < depth_south
        behind = [lane_roll(here[t], 1) for t in range(2)]
        grad = [jnp.where(open_south, here[t] - behind[t], 0.0) for t in range(2)]
        flux = face_flux(
            jnp.where(open_south, fields[k, 3], 0.0),
            behind,
            grad,
            [lane_roll(grad[t], 1) for t in range(2)],
            [lane_roll(grad[t], -1) for t in range(2)],
        )
        iso = isoneutral(
            grad,
            [centred[t] + lane_roll(centred[t], 1) for t in range(2)],
            jnp.where(iso_level < depth_south, spread, 0.0),
        )
        for t in range(2):
            net = iso[t] - flux[t]
            total[t] = total[t] + (lane_roll(net, -1) - net)
            for lane in range(LANES):
                (p_first, p_second)[t][lane, pl.ds(k * X, X), :] = total[t][:, lane * 128 : lane * 128 + 128]
        return vert, grad_down, grad_far

    def step(i, start, wait):
        first = i * UNROLL
        for u in range(UNROLL):
            if start:
                for copy in copies(first + u + AHEAD):
                    copy.start()
            if wait:
                arrive(first + u + 2)
        below = [below_flux[t] for t in range(2)]
        grads = [[grads_kept[f, t] for t in range(2)] for f in range(2)]
        tail, prev_rate = tail_out[0], tail_out[1]
        for u in range(UNROLL):
            below, grad_down, grad_far = process(first + u, below, grads[0], grads[1])
            grads = [grad_down, grad_far]
            if wait or u < UNROLL - 1:
                tail, prev_rate = eliminate(first + u, tail, prev_rate)
        for t in range(2):
            below_flux[t] = below[t]
            for f in range(2):
                grads_kept[f, t] = grads[f][t]
        tail_out[0] = tail
        tail_out[1] = prev_rate

    steps = K // UNROLL
    fed = (K - AHEAD) // UNROLL

    @pl.loop(0, fed)
    def _(i):
        step(i, True, True)

    @pl.loop(fed, steps - 1)
    def _(i):
        step(i, False, True)

    step(steps - 1, False, False)
    for t in range(2):
        for i in range(3):
            own_rows[t, i] = fields[(K - 3) * (1 - slab) + i, t]
    extra_rows[0] = fields[edge, 4]
    extra_rows[1] = fields[1, 4]
    extra_rows[2] = fields[edge, 5]
    extra_rows[3] = fields[K - 1, 6]
    for copy in column_copies:
        copy.wait()


def edge_kernel(
    east_msg, west_msg, level_msg, sea, bottom,
    p_first, p_second, inverse, carry, tail, cols, zcols, dcols, own_rows, extra_rows,
    v_first, v_second, meet_out, corner_out,
    p, rows, sems
):
    slab = lax.axis_index("lev")
    edge = (K - 1) * (1 - slab)
    inner = 30 - 29 * slab
    base = K * slab
    fetches = [
        pltpu.make_async_copy(ref, p.at[t], sems.at[t]) for t, ref in enumerate((p_first, p_second))
    ]
    for fetch in fetches:
        fetch.start()
    for t in range(2):
        for i in range(3):
            rows[t, 2 * slab + i] = own_rows[t, i]
        for i in range(2):
            rows[t, 3 * (1 - slab) + i] = level_msg[2 * t + i]

    depth = sea[...] * (bottom[...] + 1)

    level = base + lax.broadcasted_iota(jnp.int32, (K, Y), 0)
    local_row = lax.broadcasted_iota(jnp.int32, (K, Y), 0)

    def zonal_edge(q, depths, halo, courants, spreads, outer_face):
        centred = []
        for i in range(3):
            column_depth = depths[i + 1]
            pair = []
            for t in range(2):
                mine = q[t][i + 1]
                outer = halo[t][i]
                below = jnp.where(local_row == K - 1, outer, row_roll(mine, -1))
                down = jnp.where(level + 1 < column_depth, below - mine, 0.0)
                top = jnp.where(
                    (slab == 1) & (level < column_depth), mine - outer, 0.0
                )
                up = jnp.where(local_row == 0, top, row_roll(down, 1))
                pair.append(up + down)
            centred.append(pair)
        opened = [level < jnp.minimum(depths[i], depths[i + 1]) for i in range(4)]
        grads = [
            [jnp.where(opened[i], q[t][i + 1] - q[t][i], 0.0) for t in range(2)] for i in range(4)
        ]
        nets = []
        for f in range(2):
            flux = face_flux(
                jnp.where(opened[f + 1], courants[f], 0.0),
                [q[t][f + 1] for t in range(2)],
                grads[f + 1],
                grads[f],
                grads[f + 2],
            )
            iso = isoneutral(
                grads[f + 1],
                [centred[f][t] + centred[f + 1][t] for t in range(2)],
                jnp.where(opened[f + 1] & (local_row != edge) if f == outer_face else opened[f + 1], spreads[f], 0.0),
            )
            nets.append([iso[t] - flux[t] for t in range(2)])
        return nets

    def add_column(t, x, values):
        for lane in range(LANES):
            where = (t, lane, pl.ds(x, K, stride=X), slice(None))
            p[where] = p[where] + values[:, lane * 128 : lane * 128 + 128]

    def depth_row(x):
        return depth[x : x + 1]

    def near(t, x):
        return level_msg[2 * t + slab, x : x + 1, :]

    west_depths = east_msg[4 * K : 4 * K + 8, :].astype(jnp.int32)
    nets = zonal_edge(
        [
            [east_msg[(2 * t + i) * K : (2 * t + i + 1) * K, :] for i in range(2)]
            + [cols[t, i] for i in range(3)]
            for t in range(2)
        ],
        [west_depths[6:7], west_depths[7:8], depth_row(0), depth_row(1), depth_row(2)],
        [[near(t, 0), near(t, 0), near(t, 1)] for t in range(2)],
        [zcols[0], zcols[1]],
        [dcols[0], dcols[1]],
        0,
    )
    for fetch in fetches:
        fetch.wait()
    for t in range(2):
        add_column(t, 0, nets[1][t] - nets[0][t])
        add_column(t, 1, -nets[1][t])
    east_depths = west_msg[6 * K : 6 * K + 8, :].astype(jnp.int32)
    nets = zonal_edge(
        [
            [cols[t, 3 + i] for i in range(3)]
            + [west_msg[(2 * t + i) * K : (2 * t + i + 1) * K, :] for i in range(2)]
            for t in range(2)
        ],
        [depth_row(X - 3), depth_row(X - 2), depth_row(X - 1), east_depths[0:1], east_depths[1:2]],
        [[near(t, X - 2), near(t, X - 1), near(t, X - 1)] for t in range(2)],
        [zcols[2], west_msg[4 * K : 5 * K, :]],
        [dcols[2], west_msg[5 * K : 6 * K, :]],
        1,
    )
    for t in range(2):
        add_column(t, X - 2, nets[0][t])
        add_column(t, X - 1, nets[1][t] - nets[0][t])

    start = K - 3 + slab
    q = [[rows[t, i] for i in range(5)] for t in range(2)]
    grads = [
        [jnp.where(start + i + 1 < depth, q[t][i + 1] - q[t][i], 0.0) for t in range(2)]
        for i in range(4)
    ]
    other = level_msg[4]
    courant_low = jnp.where(slab == 0, other, extra_rows[1])
    above = face_flux(
        jnp.where(start + 2 < depth, extra_rows[0], 0.0),
        [q[t][1] for t in range(2)], grads[1], grads[0], grads[2],
    )
    under = face_flux(
        jnp.where(start + 3 < depth, courant_low, 0.0),
        [q[t][2] for t in range(2)], grads[2], grads[1], grads[3],
    )
    centred = [grads[1][t] + grads[2][t] for t in range(2)]
    here = [q[t][2] for t in range(2)]
    mid = start + 2
    depth_west = west_depth(depth)
    row = lax.broadcasted_iota(jnp.int32, (X, Y), 0)
    depth_west_inner = jnp.where((row >= 2) & (row <= X - 2), depth_west, 0)
    depth_south = south_depth(depth)
    spread = extra_rows[2]
    grad = [jnp.where(mid < depth_west, here[t] - row_roll(here[t], 1), 0.0) for t in range(2)]
    zonal_iso = isoneutral(
        grad,
        [centred[t] + row_roll(centred[t], 1) for t in range(2)],
        jnp.where(mid < depth_west_inner, spread, 0.0),
    )
    grad = [jnp.where(mid < depth_south, here[t] - lane_roll(here[t], 1), 0.0) for t in range(2)]
    merid_iso = isoneutral(
        grad,
        [centred[t] + lane_roll(centred[t], 1) for t in range(2)],
        jnp.where(mid < depth_south, spread, 0.0),
    )

    def add_level(t, k, values):
        for lane in range(LANES):
            where = (t, lane, pl.ds(pl.multiple_of(k * X, X), X), slice(None))
            p[where] = p[where] + values[:, lane * 128 : lane * 128 + 128]

    for t in range(2):
        change = row_roll(zonal_iso[t], -1) - zonal_iso[t]
        change = change + (lane_roll(merid_iso[t], -1) - merid_iso[t])
        add_level(t, edge, change - (under[t] - above[t]))
        add_level(t, inner, jnp.where(slab == 0, -above[t], under[t]))

    def provisional(t, k):
        rows_at = pl.ds(pl.multiple_of(k * X, X), X)
        return jnp.concatenate([p[t, lane, rows_at, :] for lane in range(LANES)], axis=1)

    def forward(j, values):
        k = jnp.where(slab == 0, j, K - 1 - j)
        inv = inverse[j]
        car = carry[j]
        new = tuple(provisional(t, k) * inv + car * values[t] for t in range(2))
        for t in range(2):
            (v_first, v_second)[t][k] = new[t]
        return new

    zero = jnp.zeros((X, Y), F32)
    values = lax.fori_loop(0, K - 1, forward, (zero, zero))
    meet_rate = jnp.where(K < depth, jnp.sqrt(jnp.where(slab == 0, extra_rows[3], other)), 0.0)
    prev_rate = tail[1]
    rest = 1.0 + prev_rate * tail[0]
    inv = 1.0 / (rest + meet_rate)
    for t in range(2):
        meet_out[t] = (provisional(t, edge) + prev_rate * values[t]) * inv
    meet_out[2] = rest * inv

    corner_out[...] = jnp.zeros_like(corner_out)
    meet_out[3] = jnp.zeros((X, Y), F32)
    own_level = base + edge
    outside = ((east_msg, K, west_depths[7:8], 0), (west_msg, 0, east_depths[0:1], X - 1))
    open_inner = jnp.where(slab == 0, K - 1, K + 1)
    open_other = jnp.where(slab == 0, K + 1, K - 1)
    for side, (msg, offset, outer_depth, x) in enumerate(outside):
        column_depth = depth_row(x)
        for t in range(2):
            at_edge = offset + 2 * t * K + edge
            outer = msg[pl.ds(at_edge, 1), :]
            outer_inner = msg[pl.ds(offset + 2 * t * K + inner, 1), :]
            meet_out[3, 2 * t + side : 2 * t + side + 1, :] = outer
            meet_out[3, 4 + 2 * t + side : 5 + 2 * t + side, :] = jnp.where(
                open_inner < outer_depth, outer - outer_inner, 0.0
            )
            mine = own_rows[t, 2 * (1 - slab), x : x + 1, :]
            mine_inner = own_rows[t, 1, x : x + 1, :]
            theirs = near(t, x)
            theirs_inner = level_msg[2 * t + 1 - slab, x : x + 1, :]
            cross = jnp.where(K < column_depth, theirs - mine, 0.0)
            corner_out[t, side : side + 1, :] = mine
            corner_out[t, 2 + side : 3 + side, :] = theirs
            corner_out[2 + t, side : side + 1, :] = cross + jnp.where(
                open_inner < column_depth, mine - mine_inner, 0.0
            )
            corner_out[2 + t, 2 + side : 3 + side, :] = (
                jnp.where(open_other < column_depth, theirs - theirs_inner, 0.0) - cross
            )
        spread_row = dcols[0, pl.ds(edge, 1), :] if side == 0 else west_msg[pl.ds(5 * K + edge, 1), :]
        meet_out[3, 8 + side : 9 + side, :] = jnp.where(
            own_level < jnp.minimum(outer_depth, column_depth), spread_row, 0.0
        )
        meet_out[3, 10 + side : 11 + side, :] = inv[x : x + 1]
        shared = jnp.where(K < outer_depth, 1.0, 0.0)
        corner_out[4, side : side + 1, :] = shared
        corner_out[4, 2 + side : 3 + side, :] = shared


def finish_kernel(v_first, v_second, ratio, mine, theirs, corner, out, u, gathered, change, sems):
    slab = lax.axis_index("lev")
    for i in range(6):
        gathered[i, 0:2, :] = mine[3, 2 * i : 2 * i + 2, :]
        gathered[i, 2:4, :] = theirs[3, 2 * i : 2 * i + 2, :]
        gathered[i, 4:6, :] = theirs[3, 2 * i : 2 * i + 2, :]
        gathered[i, 6:8, :] = mine[3, 2 * i : 2 * i + 2, :]
    grad = []
    vert = []
    for t in range(2):
        outer = gathered[t]
        other = row_roll(outer, 4)
        grad.append(outer - corner[t])
        vert.append(corner[2 + t] + gathered[2 + t] + corner[4] * (other - outer))
    flux = isoneutral(grad, vert, gathered[4])
    change[...] = jnp.zeros_like(change)
    for t in range(2):
        moved = flux[t] * gathered[5]
        for i in range(2):
            change[i, t, 0:1, :] = moved[2 * i : 2 * i + 1]
            change[i, t, X - 1 : X, :] = moved[2 * i + 1 : 2 * i + 2]
    own_tail = mine[2]
    own_ratio = 1.0 - own_tail
    scale = reciprocal(own_tail + own_ratio * theirs[2])
    last = tuple(
        (mine[t] + change[0, t] + own_ratio * (theirs[t] + change[1, t])) * scale for t in range(2)
    )
    edge = (K - 1) * (1 - slab)

    def copies(k):
        return [pltpu.make_async_copy(u.at[:, k], out.at[:, :, k, :], sems.at[k])]

    for t in range(2):
        u[t, edge] = last[t]
    for copy in copies(edge):
        copy.start()

    def backward(i, values):
        j = K - 2 - i
        k = jnp.where(slab == 0, j, K - 1 - j)
        rat = ratio[j]
        new = tuple(v[k] + rat * values[t] for t, v in enumerate((v_first, v_second)))
        for t in range(2):
            u[t, k] = new[t]
        for copy in copies(k):
            copy.start()
        return new

    lax.fori_loop(0, K - 1, backward, last)

    @pl.loop(0, K)
    def _(k):
        for copy in copies(k):
            copy.wait()


def shape(*dims):
    return jax.ShapeDtypeStruct(dims, F32)


def params(mib):
    return pltpu.CompilerParams(vmem_limit_bytes=mib * 1024 * 1024)


def local(
    tracers, zonal, merid, vertical, diffusivity, turbulence, sea, bottom
):
    count = lax.axis_size("tile")
    east_msg, west_msg, level_msg = pl.pallas_call(
        pack_kernel,
        name="pack",
        in_specs=[any_spec()] * 7,
        out_specs=[vmem_spec()] * 3,
        out_shape=[shape(4 * K + 8, Y), shape(6 * K + 8, Y), shape(5, X, Y)],
        scratch_shapes=[
            pltpu.VMEM((X, Y), F32), pltpu.VMEM((2, X, Y), jnp.int32), pltpu.SemaphoreType.DMA((24,))
        ],
        compiler_params=params(60),
    )(tracers, zonal, vertical, diffusivity, turbulence, sea, bottom)

    eastward = [(i, (i + 1) % count) for i in range(count)]
    east_in = lax.ppermute(east_msg, "tile", eastward)
    west_in = lax.ppermute(west_msg, "tile", [(b, a) for a, b in eastward])
    level_in = lax.ppermute(level_msg, "lev", [(0, 1), (1, 0)])

    p_first, p_second, inverse, carry, ratio, tail, *pieces = pl.pallas_call(
        interior_kernel,
        name="interior",
        in_specs=[any_spec()] * 8,
        out_specs=[vmem_spec()] * 11,
        out_shape=[
            shape(LANES, K * X, 128), shape(LANES, K * X, 128), shape(K, X, Y), shape(K, X, Y), shape(K, X, Y),
            shape(2, X, Y),
            shape(2, 6, K, Y), shape(3, K, Y), shape(3, K, Y), shape(2, 3, X, Y), shape(4, X, Y),
        ],
        scratch_shapes=[
            pltpu.VMEM((K, 7, X, Y), F32),
            pltpu.VMEM((2, X, Y), F32),
            pltpu.VMEM((2, 2, X, Y), F32),
            pltpu.VMEM((2, X, Y), jnp.int32),
            pltpu.SemaphoreType.DMA((K,)),
            pltpu.SemaphoreType.DMA((20,)),
        ],
        compiler_params=params(49),
        cost_estimate=pl.CostEstimate(flops=50_000_000, bytes_accessed=40_000_000, transcendentals=0),
    )(tracers, zonal, merid, vertical, diffusivity, turbulence, sea, bottom)

    v_first, v_second, meet, corner = pl.pallas_call(
        edge_kernel,
        name="edges",
        in_specs=[vmem_spec()] * 15,
        out_specs=[vmem_spec()] * 4,
        out_shape=[shape(K, X, Y), shape(K, X, Y), shape(4, X, Y), shape(5, 8, Y)],
        scratch_shapes=[
            pltpu.VMEM((2, LANES, K * X, 128), F32),
            pltpu.VMEM((2, 5, X, Y), F32),
            pltpu.SemaphoreType.DMA((2,)),
        ],
        compiler_params=params(46),
    )(east_in, west_in, level_in, sea, bottom, p_first, p_second, inverse, carry, tail, *pieces)

    meet_in = lax.ppermute(meet, "lev", [(0, 1), (1, 0)])
    return pl.pallas_call(
        finish_kernel,
        name="finish",
        in_specs=[vmem_spec()] * 6,
        out_specs=any_spec(),
        out_shape=shape(2, X, K, Y),
        scratch_shapes=[
            pltpu.VMEM((2, K, X, Y), F32),
            pltpu.VMEM((6, 8, Y), F32),
            pltpu.VMEM((2, 2, X, Y), F32),
            pltpu.SemaphoreType.DMA((K,)),
        ],
        compiler_params=params(46),
    )(v_first, v_second, ratio, meet, meet_in, corner)


def solution(mesh):
    return jax.shard_map(
        local,
        mesh=mesh,
        in_specs=(
            P(None, "tile", "lev", None),
            P("tile", "lev", None),
            P("tile", "lev", None),
            P("tile", "lev", None),
            P("tile", "lev", None),
            P("tile", "lev", None),
            P("tile", None),
            P("tile", None),
        ),
        out_specs=P(None, "tile", "lev", None),
        check_vma=False,
    )
```

```python
import jax
import jax.numpy as jnp
from jax import lax
from jax.experimental import pallas as pl
from jax.experimental.pallas import tpu as pltpu
from jax.sharding import PartitionSpec as P

thermal_coef = 0.2
haline_coef = 0.8
taper_eps = 0.05

X = 16
K = 32
Y = 384
LANES = 3
UNROLL = 2
AHEAD = 24
FAR = 1 << 20
F32 = jnp.float32


def any_spec():
    return pl.BlockSpec(memory_space=pl.ANY)


def vmem_spec():
    return pl.BlockSpec(memory_space=pltpu.VMEM)


def face_flux(courant, behind, grad, back, front):
    half = 0.5 * courant
    half_speed = jnp.abs(half)
    weight = half_speed - 2.0 * half_speed * half_speed
    lag = half - half_speed
    forward = courant > 0.0
    fluxes = []
    for t in range(2):
        upwind = jnp.where(forward, back[t], front[t])
        low = jnp.minimum(grad[t], 0.0)
        high = jnp.maximum(grad[t], 0.0)
        double = jnp.minimum(jnp.maximum(upwind + upwind, low), high)
        excess = jnp.minimum(jnp.maximum(upwind - grad[t], low), high)
        fluxes.append(courant * behind[t] + lag * grad[t] + weight * (double + excess))
    return fluxes


def reciprocal(values):
    guess = pl.reciprocal(values, approx=True)
    return guess * (2.0 - values * guess)


def isoneutral(grad, vert, coeff):
    ratio = haline_coef / thermal_coef
    dens_side = ratio * grad[1] - grad[0]
    dens_vert = ratio * vert[1] - vert[0]
    floor = 16.0 * taper_eps / (thermal_coef * thermal_coef)
    slope = dens_side * dens_vert * reciprocal(dens_vert * dens_vert + floor)
    return [coeff * (grad[t] - slope * vert[t]) for t in range(2)]


def lane_roll(values, shift):
    return pltpu.roll(values, shift % Y, 1)


def row_roll(values, shift):
    return pltpu.roll(values, shift % values.shape[0], 0)


def south_depth(depth):
    lane = lax.broadcasted_iota(jnp.int32, depth.shape, 1)
    return jnp.where(lane == 0, 0, jnp.minimum(depth, lane_roll(depth, 1)))


def west_depth(depth):
    return jnp.minimum(depth, row_roll(depth, 1))


def pack_kernel(
    tracers, zonal, vertical, diffusivity, turbulence, sea, bottom,
    east_msg, west_msg, level_msg, depth_rows, column, sems
):
    slab = lax.axis_index("lev")
    first = (K - 2) * (1 - slab)
    shapes = [
        pltpu.make_async_copy(ref, column.at[i], sems.at[20 + i]) for i, ref in enumerate((sea, bottom))
    ]
    for copy in shapes:
        copy.start()
    copies = []

    def add(src, dst):
        copies.append(pltpu.make_async_copy(src, dst, sems.at[len(copies)]))
        copies[-1].start()

    for t in range(2):
        for i in range(2):
            rows = pl.ds((2 * t + i) * K, K)
            add(tracers.at[t, X - 2 + i], east_msg.at[rows])
            add(tracers.at[t, i], west_msg.at[rows])
            add(tracers.at[t, :, first + i, :], level_msg.at[2 * t + i])
    add(zonal.at[0], west_msg.at[pl.ds(4 * K, K)])
    add(diffusivity.at[0], west_msg.at[pl.ds(5 * K, K)])
    fifth = len(copies)
    upper = pltpu.make_async_copy(turbulence.at[:, K - 1, :], level_msg.at[4], sems.at[fifth])
    lower = pltpu.make_async_copy(vertical.at[:, 0, :], level_msg.at[4], sems.at[fifth])

    @pl.when(slab == 0)
    def _():
        upper.start()

    @pl.when(slab == 1)
    def _():
        lower.start()

    for copy in shapes:
        copy.wait()
    depth_rows[...] = (column[0] * (column[1] + 1)).astype(F32)
    last = [
        pltpu.make_async_copy(depth_rows.at[pl.ds(8, 8)], east_msg.at[pl.ds(4 * K, 8)], sems.at[fifth + 1]),
        pltpu.make_async_copy(depth_rows.at[pl.ds(0, 8)], west_msg.at[pl.ds(6 * K, 8)], sems.at[fifth + 2]),
    ]
    for copy in last:
        copy.start()
    upper.wait()
    for copy in copies + last:
        copy.wait()


def interior_kernel(
    tracers, zonal, merid, vertical, diffusivity, turbulence, sea, bottom,
    p_first, p_second, inverse_out, carry_out, ratio_out, tail_out, cols, zcols, dcols, own_rows, extra_rows,
    fields, below_flux, grads_kept, column, sems, col_sems
):
    slab = lax.axis_index("lev")
    edge = (K - 1) * (1 - slab)
    base = K * slab

    def copies(k):
        turned = jnp.where(slab == 0, k, jnp.maximum(K - 2 - k, 0))
        pairs = [
            (tracers.at[:, :, k, :], fields.at[k, 0:2]),
            (zonal.at[:, k, :], fields.at[k, 2]),
            (merid.at[:, k, :], fields.at[k, 3]),
            (vertical.at[:, k, :], fields.at[k, 4]),
            (diffusivity.at[:, k, :], fields.at[k, 5]),
            (turbulence.at[:, turned, :], fields.at[k, 6]),
        ]
        return [pltpu.make_async_copy(a, b, sems.at[k]) for a, b in pairs]

    def arrive(k):
        pltpu.make_async_copy(fields.at[k], fields.at[k], sems.at[k]).wait()

    shapes = [
        pltpu.make_async_copy(ref, column.at[i], col_sems.at[18 + i]) for i, ref in enumerate((sea, bottom))
    ]
    for copy in shapes:
        copy.start()
    for k in range(AHEAD):
        for copy in copies(k):
            copy.start()
    for copy in shapes:
        copy.wait()

    depth = column[0] * (column[1] + 1)
    depth_west = west_depth(depth)
    row = lax.broadcasted_iota(jnp.int32, (X, Y), 0)
    depth_west_inner = jnp.where((row >= 2) & (row <= X - 2), depth_west, 0)
    depth_south = south_depth(depth)
    below_flux[...] = jnp.zeros_like(below_flux)
    tail_out[...] = jnp.zeros_like(tail_out)
    grads_kept[0] = jnp.zeros((2, X, Y), F32)

    for k in range(2):
        arrive(k)
    column_copies = []

    def add(src, dst):
        column_copies.append(pltpu.make_async_copy(src, dst, col_sems.at[len(column_copies)]))
        column_copies[-1].start()

    for i, x in enumerate((0, 1, 2, X - 3, X - 2, X - 1)):
        for t in range(2):
            add(tracers.at[t, x], cols.at[t, i])
    for i, x in enumerate((0, 1, X - 1)):
        add(zonal.at[x], zcols.at[i])
        add(diffusivity.at[x], dcols.at[i])
    for t in range(2):
        grads_kept[1, t] = jnp.where(base + 1 < depth, fields[1, t] - fields[0, t], 0.0)

    def eliminate(j, tail, prev_rate):
        face = jnp.where(slab == 0, j + 1, 2 * K - 1 - j)
        turb = fields[j, 6]
        next_rate = jnp.where(face < depth, turb * lax.rsqrt(turb), 0.0)
        rest = 1.0 + prev_rate * tail
        inverse = reciprocal(rest + next_rate)
        inverse_out[j] = inverse
        carry_out[j] = prev_rate * inverse
        ratio_out[j] = next_rate * inverse
        return rest * inverse, next_rate

    def process(k, below, grad_up, grad_down):
        ahead = jnp.minimum(k + 2, K - 1)
        level = base + k
        down = jnp.minimum(k + 1, K - 1)
        here = [fields[k, t] for t in range(2)]
        next_row = [fields[down, t] for t in range(2)]
        open_far = jnp.where(k < K - 2, level + 2, FAR) < depth
        grad_far = [jnp.where(open_far, fields[ahead, t] - next_row[t], 0.0) for t in range(2)]
        centred = [grad_up[t] + grad_down[t] for t in range(2)]
        known = jnp.where(slab == 0, k < K - 2, k > 0)
        open_flux = jnp.where(known, level + 1, FAR) < depth
        down_courant = jnp.where(open_flux, fields[down, 4], 0.0)
        vert = face_flux(down_courant, here, grad_down, grad_up, grad_far)
        total = []
        for t in range(2):
            total.append(here[t] + below[t] - vert[t])
        iso_level = jnp.where(k == edge, FAR, level)
        spread = fields[k, 5]

        open_west = level < depth_west
        behind = [row_roll(here[t], 1) for t in range(2)]
        grad = [jnp.where(open_west, here[t] - behind[t], 0.0) for t in range(2)]
        flux = face_flux(
            jnp.where(level < depth_west_inner, fields[k, 2], 0.0),
            behind,
            grad,
            [row_roll(grad[t], 1) for t in range(2)],
            [row_roll(grad[t], -1) for t in range(2)],
        )
        iso = isoneutral(
            grad,
            [centred[t] + row_roll(centred[t], 1) for t in range(2)],
            jnp.where(iso_level < depth_west_inner, spread, 0.0),
        )
        for t in range(2):
            net = iso[t] - flux[t]
            total[t] = total[t] + (row_roll(net, -1) - net)

        open_south = level < depth_south
        behind = [lane_roll(here[t], 1) for t in range(2)]
        grad = [jnp.where(open_south, here[t] - behind[t], 0.0) for t in range(2)]
        flux = face_flux(
            jnp.where(open_south, fields[k, 3], 0.0),
            behind,
            grad,
            [lane_roll(grad[t], 1) for t in range(2)],
            [lane_roll(grad[t], -1) for t in range(2)],
        )
        iso = isoneutral(
            grad,
            [centred[t] + lane_roll(centred[t], 1) for t in range(2)],
            jnp.where(iso_level < depth_south, spread, 0.0),
        )
        for t in range(2):
            net = iso[t] - flux[t]
            total[t] = total[t] + (lane_roll(net, -1) - net)
            for lane in range(LANES):
                (p_first, p_second)[t][lane, pl.ds(k * X, X), :] = total[t][:, lane * 128 : lane * 128 + 128]
        return vert, grad_down, grad_far

    def step(i, start, wait):
        first = i * UNROLL
        for u in range(UNROLL):
            if start:
                for copy in copies(first + u + AHEAD):
                    copy.start()
            if wait:
                arrive(first + u + 2)
        below = [below_flux[t] for t in range(2)]
        grads = [[grads_kept[f, t] for t in range(2)] for f in range(2)]
        tail, prev_rate = tail_out[0], tail_out[1]
        for u in range(UNROLL):
            below, grad_down, grad_far = process(first + u, below, grads[0], grads[1])
            grads = [grad_down, grad_far]
            if wait or u < UNROLL - 1:
                tail, prev_rate = eliminate(first + u, tail, prev_rate)
        for t in range(2):
            below_flux[t] = below[t]
            for f in range(2):
                grads_kept[f, t] = grads[f][t]
        tail_out[0] = tail
        tail_out[1] = prev_rate

    steps = K // UNROLL
    fed = (K - AHEAD) // UNROLL

    @pl.loop(0, fed)
    def _(i):
        step(i, True, True)

    @pl.loop(fed, steps - 1)
    def _(i):
        step(i, False, True)

    step(steps - 1, False, False)
    for t in range(2):
        for i in range(3):
            own_rows[t, i] = fields[(K - 3) * (1 - slab) + i, t]
    extra_rows[0] = fields[edge, 4]
    extra_rows[1] = fields[1, 4]
    extra_rows[2] = fields[edge, 5]
    extra_rows[3] = fields[K - 1, 6]
    for copy in column_copies:
        copy.wait()


def edge_kernel(
    east_msg, west_msg, level_msg, sea, bottom,
    p_first, p_second, inverse, carry, tail, cols, zcols, dcols, own_rows, extra_rows,
    v_first, v_second, meet_out, corner_out,
    p, rows, sems
):
    slab = lax.axis_index("lev")
    edge = (K - 1) * (1 - slab)
    inner = 30 - 29 * slab
    base = K * slab
    fetches = [
        pltpu.make_async_copy(ref, p.at[t], sems.at[t]) for t, ref in enumerate((p_first, p_second))
    ]
    for fetch in fetches:
        fetch.start()
    for t in range(2):
        for i in range(3):
            rows[t, 2 * slab + i] = own_rows[t, i]
        for i in range(2):
            rows[t, 3 * (1 - slab) + i] = level_msg[2 * t + i]

    depth = sea[...] * (bottom[...] + 1)

    level = base + lax.broadcasted_iota(jnp.int32, (K, Y), 0)
    local_row = lax.broadcasted_iota(jnp.int32, (K, Y), 0)

    def zonal_edge(q, depths, halo, courants, spreads, outer_face):
        centred = []
        for i in range(3):
            column_depth = depths[i + 1]
            pair = []
            for t in range(2):
                mine = q[t][i + 1]
                outer = halo[t][i]
                below = jnp.where(local_row == K - 1, outer, row_roll(mine, -1))
                down = jnp.where(level + 1 < column_depth, below - mine, 0.0)
                top = jnp.where(
                    (slab == 1) & (level < column_depth), mine - outer, 0.0
                )
                up = jnp.where(local_row == 0, top, row_roll(down, 1))
                pair.append(up + down)
            centred.append(pair)
        opened = [level < jnp.minimum(depths[i], depths[i + 1]) for i in range(4)]
        grads = [
            [jnp.where(opened[i], q[t][i + 1] - q[t][i], 0.0) for t in range(2)] for i in range(4)
        ]
        nets = []
        for f in range(2):
            flux = face_flux(
                jnp.where(opened[f + 1], courants[f], 0.0),
                [q[t][f + 1] for t in range(2)],
                grads[f + 1],
                grads[f],
                grads[f + 2],
            )
            iso = isoneutral(
                grads[f + 1],
                [centred[f][t] + centred[f + 1][t] for t in range(2)],
                jnp.where(opened[f + 1] & (local_row != edge) if f == outer_face else opened[f + 1], spreads[f], 0.0),
            )
            nets.append([iso[t] - flux[t] for t in range(2)])
        return nets

    def add_column(t, x, values):
        for lane in range(LANES):
            where = (t, lane, pl.ds(x, K, stride=X), slice(None))
            p[where] = p[where] + values[:, lane * 128 : lane * 128 + 128]

    def depth_row(x):
        return depth[x : x + 1]

    def near(t, x):
        return level_msg[2 * t + slab, x : x + 1, :]

    west_depths = east_msg[4 * K : 4 * K + 8, :].astype(jnp.int32)
    nets = zonal_edge(
        [
            [east_msg[(2 * t + i) * K : (2 * t + i + 1) * K, :] for i in range(2)]
            + [cols[t, i] for i in range(3)]
            for t in range(2)
        ],
        [west_depths[6:7], west_depths[7:8], depth_row(0), depth_row(1), depth_row(2)],
        [[near(t, 0), near(t, 0), near(t, 1)] for t in range(2)],
        [zcols[0], zcols[1]],
        [dcols[0], dcols[1]],
        0,
    )
    for fetch in fetches:
        fetch.wait()
    for t in range(2):
        add_column(t, 0, nets[1][t] - nets[0][t])
        add_column(t, 1, -nets[1][t])
    east_depths = west_msg[6 * K : 6 * K + 8, :].astype(jnp.int32)
    nets = zonal_edge(
        [
            [cols[t, 3 + i] for i in range(3)]
            + [west_msg[(2 * t + i) * K : (2 * t + i + 1) * K, :] for i in range(2)]
            for t in range(2)
        ],
        [depth_row(X - 3), depth_row(X - 2), depth_row(X - 1), east_depths[0:1], east_depths[1:2]],
        [[near(t, X - 2), near(t, X - 1), near(t, X - 1)] for t in range(2)],
        [zcols[2], west_msg[4 * K : 5 * K, :]],
        [dcols[2], west_msg[5 * K : 6 * K, :]],
        1,
    )
    for t in range(2):
        add_column(t, X - 2, nets[0][t])
        add_column(t, X - 1, nets[1][t] - nets[0][t])

    start = K - 3 + slab
    q = [[rows[t, i] for i in range(5)] for t in range(2)]
    grads = [
        [jnp.where(start + i + 1 < depth, q[t][i + 1] - q[t][i], 0.0) for t in range(2)]
        for i in range(4)
    ]
    other = level_msg[4]
    courant_low = jnp.where(slab == 0, other, extra_rows[1])
    above = face_flux(
        jnp.where(start + 2 < depth, extra_rows[0], 0.0),
        [q[t][1] for t in range(2)], grads[1], grads[0], grads[2],
    )
    under = face_flux(
        jnp.where(start + 3 < depth, courant_low, 0.0),
        [q[t][2] for t in range(2)], grads[2], grads[1], grads[3],
    )
    centred = [grads[1][t] + grads[2][t] for t in range(2)]
    here = [q[t][2] for t in range(2)]
    mid = start + 2
    depth_west = west_depth(depth)
    row = lax.broadcasted_iota(jnp.int32, (X, Y), 0)
    depth_west_inner = jnp.where((row >= 2) & (row <= X - 2), depth_west, 0)
    depth_south = south_depth(depth)
    spread = extra_rows[2]
    grad = [jnp.where(mid < depth_west, here[t] - row_roll(here[t], 1), 0.0) for t in range(2)]
    zonal_iso = isoneutral(
        grad,
        [centred[t] + row_roll(centred[t], 1) for t in range(2)],
        jnp.where(mid < depth_west_inner, spread, 0.0),
    )
    grad = [jnp.where(mid < depth_south, here[t] - lane_roll(here[t], 1), 0.0) for t in range(2)]
    merid_iso = isoneutral(
        grad,
        [centred[t] + lane_roll(centred[t], 1) for t in range(2)],
        jnp.where(mid < depth_south, spread, 0.0),
    )

    def add_level(t, k, values):
        for lane in range(LANES):
            where = (t, lane, pl.ds(pl.multiple_of(k * X, X), X), slice(None))
            p[where] = p[where] + values[:, lane * 128 : lane * 128 + 128]

    for t in range(2):
        change = row_roll(zonal_iso[t], -1) - zonal_iso[t]
        change = change + (lane_roll(merid_iso[t], -1) - merid_iso[t])
        add_level(t, edge, change - (under[t] - above[t]))
        add_level(t, inner, jnp.where(slab == 0, -above[t], under[t]))

    def provisional(t, k):
        rows_at = pl.ds(pl.multiple_of(k * X, X), X)
        return jnp.concatenate([p[t, lane, rows_at, :] for lane in range(LANES)], axis=1)

    def forward(j, values):
        k = jnp.where(slab == 0, j, K - 1 - j)
        inv = inverse[j]
        car = carry[j]
        new = tuple(provisional(t, k) * inv + car * values[t] for t in range(2))
        for t in range(2):
            (v_first, v_second)[t][k] = new[t]
        return new

    zero = jnp.zeros((X, Y), F32)
    values = lax.fori_loop(0, K - 1, forward, (zero, zero))
    meet_rate = jnp.where(K < depth, jnp.sqrt(jnp.where(slab == 0, extra_rows[3], other)), 0.0)
    prev_rate = tail[1]
    rest = 1.0 + prev_rate * tail[0]
    inv = 1.0 / (rest + meet_rate)
    for t in range(2):
        meet_out[t] = (provisional(t, edge) + prev_rate * values[t]) * inv
    meet_out[2] = rest * inv

    corner_out[...] = jnp.zeros_like(corner_out)
    meet_out[3] = jnp.zeros((X, Y), F32)
    own_level = base + edge
    outside = ((east_msg, K, west_depths[7:8], 0), (west_msg, 0, east_depths[0:1], X - 1))
    open_inner = jnp.where(slab == 0, K - 1, K + 1)
    open_other = jnp.where(slab == 0, K + 1, K - 1)
    for side, (msg, offset, outer_depth, x) in enumerate(outside):
        column_depth = depth_row(x)
        for t in range(2):
            at_edge = offset + 2 * t * K + edge
            outer = msg[pl.ds(at_edge, 1), :]
            outer_inner = msg[pl.ds(offset + 2 * t * K + inner, 1), :]
            meet_out[3, 2 * t + side : 2 * t + side + 1, :] = outer
            meet_out[3, 4 + 2 * t + side : 5 + 2 * t + side, :] = jnp.where(
                open_inner < outer_depth, outer - outer_inner, 0.0
            )
            mine = own_rows[t, 2 * (1 - slab), x : x + 1, :]
            mine_inner = own_rows[t, 1, x : x + 1, :]
            theirs = near(t, x)
            theirs_inner = level_msg[2 * t + 1 - slab, x : x + 1, :]
            cross = jnp.where(K < column_depth, theirs - mine, 0.0)
            corner_out[t, side : side + 1, :] = mine
            corner_out[t, 2 + side : 3 + side, :] = theirs
            corner_out[2 + t, side : side + 1, :] = cross + jnp.where(
                open_inner < column_depth, mine - mine_inner, 0.0
            )
            corner_out[2 + t, 2 + side : 3 + side, :] = (
                jnp.where(open_other < column_depth, theirs - theirs_inner, 0.0) - cross
            )
        spread_row = dcols[0, pl.ds(edge, 1), :] if side == 0 else west_msg[pl.ds(5 * K + edge, 1), :]
        meet_out[3, 8 + side : 9 + side, :] = jnp.where(
            own_level < jnp.minimum(outer_depth, column_depth), spread_row, 0.0
        )
        meet_out[3, 10 + side : 11 + side, :] = inv[x : x + 1]
        shared = jnp.where(K < outer_depth, 1.0, 0.0)
        corner_out[4, side : side + 1, :] = shared
        corner_out[4, 2 + side : 3 + side, :] = shared


def finish_kernel(v_first, v_second, ratio, mine, theirs, corner, out, u, gathered, change, sems):
    slab = lax.axis_index("lev")
    for i in range(6):
        gathered[i, 0:2, :] = mine[3, 2 * i : 2 * i + 2, :]
        gathered[i, 2:4, :] = theirs[3, 2 * i : 2 * i + 2, :]
        gathered[i, 4:6, :] = theirs[3, 2 * i : 2 * i + 2, :]
        gathered[i, 6:8, :] = mine[3, 2 * i : 2 * i + 2, :]
    grad = []
    vert = []
    for t in range(2):
        outer = gathered[t]
        other = row_roll(outer, 4)
        grad.append(outer - corner[t])
        vert.append(corner[2 + t] + gathered[2 + t] + corner[4] * (other - outer))
    flux = isoneutral(grad, vert, gathered[4])
    change[...] = jnp.zeros_like(change)
    for t in range(2):
        moved = flux[t] * gathered[5]
        for i in range(2):
            change[i, t, 0:1, :] = moved[2 * i : 2 * i + 1]
            change[i, t, X - 1 : X, :] = moved[2 * i + 1 : 2 * i + 2]
    own_tail = mine[2]
    own_ratio = 1.0 - own_tail
    scale = reciprocal(own_tail + own_ratio * theirs[2])
    last = tuple(
        (mine[t] + change[0, t] + own_ratio * (theirs[t] + change[1, t])) * scale for t in range(2)
    )
    edge = (K - 1) * (1 - slab)

    def copies(k):
        return [pltpu.make_async_copy(u.at[:, k], out.at[:, :, k, :], sems.at[k])]

    for t in range(2):
        u[t, edge] = last[t]
    for copy in copies(edge):
        copy.start()

    def backward(i, values):
        j = K - 2 - i
        k = jnp.where(slab == 0, j, K - 1 - j)
        rat = ratio[j]
        new = tuple(v[k] + rat * values[t] for t, v in enumerate((v_first, v_second)))
        for t in range(2):
            u[t, k] = new[t]
        for copy in copies(k):
            copy.start()
        return new

    lax.fori_loop(0, K - 1, backward, last)

    @pl.loop(0, K)
    def _(k):
        for copy in copies(k):
            copy.wait()


def shape(*dims):
    return jax.ShapeDtypeStruct(dims, F32)


def params(mib):
    return pltpu.CompilerParams(vmem_limit_bytes=mib * 1024 * 1024)


def local(
    tracers, zonal, merid, vertical, diffusivity, turbulence, sea, bottom
):
    count = lax.axis_size("tile")
    east_msg, west_msg, level_msg = pl.pallas_call(
        pack_kernel,
        name="pack",
        in_specs=[any_spec()] * 7,
        out_specs=[vmem_spec()] * 3,
        out_shape=[shape(4 * K + 8, Y), shape(6 * K + 8, Y), shape(5, X, Y)],
        scratch_shapes=[
            pltpu.VMEM((X, Y), F32), pltpu.VMEM((2, X, Y), jnp.int32), pltpu.SemaphoreType.DMA((24,))
        ],
        compiler_params=params(60),
    )(tracers, zonal, vertical, diffusivity, turbulence, sea, bottom)

    eastward = [(i, (i + 1) % count) for i in range(count)]
    east_in = lax.ppermute(east_msg, "tile", eastward)
    west_in = lax.ppermute(west_msg, "tile", [(b, a) for a, b in eastward])
    level_in = lax.ppermute(level_msg, "lev", [(0, 1), (1, 0)])

    p_first, p_second, inverse, carry, ratio, tail, *pieces = pl.pallas_call(
        interior_kernel,
        name="interior",
        in_specs=[any_spec()] * 8,
        out_specs=[vmem_spec()] * 11,
        out_shape=[
            shape(LANES, K * X, 128), shape(LANES, K * X, 128), shape(K, X, Y), shape(K, X, Y), shape(K, X, Y),
            shape(2, X, Y),
            shape(2, 6, K, Y), shape(3, K, Y), shape(3, K, Y), shape(2, 3, X, Y), shape(4, X, Y),
        ],
        scratch_shapes=[
            pltpu.VMEM((K, 7, X, Y), F32),
            pltpu.VMEM((2, X, Y), F32),
            pltpu.VMEM((2, 2, X, Y), F32),
            pltpu.VMEM((2, X, Y), jnp.int32),
            pltpu.SemaphoreType.DMA((K,)),
            pltpu.SemaphoreType.DMA((20,)),
        ],
        compiler_params=params(49),
        cost_estimate=pl.CostEstimate(flops=50_000_000, bytes_accessed=40_000_000, transcendentals=0),
    )(tracers, zonal, merid, vertical, diffusivity, turbulence, sea, bottom)

    v_first, v_second, meet, corner = pl.pallas_call(
        edge_kernel,
        name="edges",
        in_specs=[vmem_spec()] * 15,
        out_specs=[vmem_spec()] * 4,
        out_shape=[shape(K, X, Y), shape(K, X, Y), shape(4, X, Y), shape(5, 8, Y)],
        scratch_shapes=[
            pltpu.VMEM((2, LANES, K * X, 128), F32),
            pltpu.VMEM((2, 5, X, Y), F32),
            pltpu.SemaphoreType.DMA((2,)),
        ],
        compiler_params=params(46),
    )(east_in, west_in, level_in, sea, bottom, p_first, p_second, inverse, carry, tail, *pieces)

    meet_in = lax.ppermute(meet, "lev", [(0, 1), (1, 0)])
    return pl.pallas_call(
        finish_kernel,
        name="finish",
        in_specs=[vmem_spec()] * 6,
        out_specs=any_spec(),
        out_shape=shape(2, X, K, Y),
        scratch_shapes=[
            pltpu.VMEM((2, K, X, Y), F32),
            pltpu.VMEM((6, 8, Y), F32),
            pltpu.VMEM((2, 2, X, Y), F32),
            pltpu.SemaphoreType.DMA((K,)),
        ],
        compiler_params=params(46),
    )(v_first, v_second, ratio, meet, meet_in, corner)


def solution(mesh):
    return jax.shard_map(
        local,
        mesh=mesh,
        in_specs=(
            P(None, "tile", "lev", None),
            P("tile", "lev", None),
            P("tile", "lev", None),
            P("tile", "lev", None),
            P("tile", "lev", None),
            P("tile", "lev", None),
            P("tile", None),
            P("tile", None),
        ),
        out_specs=P(None, "tile", "lev", None),
        check_vma=False,
    )
```
